32 devices in a mesh: section: 2 (over x), replica: 4 (over z), shard: 4 (over y, core).
Axes of the slice: x: 2, y: 2, z: 4, core: 2. Of those that a mesh axis runs over, the one named last changes fastest.
Arguments:
- ends: bfloat16 [2, 2, 4, 2048, 576], P('section', None, 'replica', 'shard'), may hold values from -6 to 6
- attn_norm: bfloat16 [2, 576], P('section', 'shard'), may hold values from 0.5 to 1.5
- w_query: bfloat16 [2, 576, 576], P('section', 'shard'), may hold values from -0.25 to 0.25
- w_key: bfloat16 [2, 576, 192], P('section', 'shard'), may hold values from -0.25 to 0.25
- w_value: bfloat16 [2, 576, 192], P('section', 'shard'), may hold values from -0.25 to 0.25
- w_out: bfloat16 [2, 576, 576], P('section', 'shard'), may hold values from -1.5 to 1.5
- ffn_norm: bfloat16 [2, 576], P('section', 'shard'), may hold values from 0.5 to 1.5
- w_gate: bfloat16 [2, 576, 1536], P('section', 'shard'), may hold values from -0.25 to 0.25
- w_up: bfloat16 [2, 576, 1536], P('section', 'shard'), may hold values from -0.25 to 0.25
- w_down: bfloat16 [2, 1536, 576], P('section', 'shard'), may hold values from -0.15625 to 0.15625
Outputs:
- ends_out: float32 [2, 2, 4, 2048, 576], P('section', None, 'replica', 'shard')
- grad_attn_norm: float32 [2, 576], P('section', 'shard')
- grad_query: float32 [2, 576, 576], P('section', 'shard')
- grad_key: float32 [2, 576, 192], P('section', 'shard')
- grad_value: float32 [2, 576, 192], P('section', 'shard')
- grad_out: float32 [2, 576, 576], P('section', 'shard')
- grad_ffn_norm: float32 [2, 576], P('section', 'shard')
- grad_gate: float32 [2, 576, 1536], P('section', 'shard')
- grad_up: float32 [2, 576, 1536], P('section', 'shard')
- grad_down: float32 [2, 1536, 576], P('section', 'shard')
The draws below stay inside these ranges and needn't reach their ends.
All inputs are finite; a program needn't handle non-finite values.
Results may differ from the reference program's by a relative error of at most 0.034.
Values may be sent and summed in bfloat16 or wider, within the bound.
A program may use at most 192 MiB of HBM per device.

```python
import jax
import jax.numpy as jnp
from jax import lax

D = 576
HEADS = 9
KV_HEADS = 3
HEAD = 64
FF = 1536
LEN = 2048
MB = 2
SEQS = 4
N_SECTION = 2


def shard_levels(own_key, dims, cuts, smallest, high):
    def one(axis_at, shards_of):
        steps = jax.random.uniform(jax.random.fold_in(jax.random.fold_in(own_key, 6), axis_at), (shards_of,), jnp.float32, smallest / len(cuts), high / len(cuts))
        return jnp.repeat(jnp.exp(steps), dims[axis_at] // shards_of).reshape((-1,) + (1,) * (len(dims) - axis_at - 1))

    gain = one(*cuts[0])
    for cut in cuts[1:]:
        gain = gain * one(*cut)
    return gain


def noise(rng, shape, deviation, limit, pieces=(), kind=jnp.bfloat16):
    values = jax.random.normal(rng, shape, jnp.float32) * deviation
    if len(pieces) > 0:
        values = shard_levels(rng, shape, pieces, -0.22, 0.18) * values
    return jnp.clip(values, min=-limit, max=limit).astype(kind)


def setup_inputs(seed: int = 0) -> dict:
    key_of = jax.random.split(jax.random.key(seed), 11)
    return {
        "ends": noise(key_of[0], (2, MB, SEQS, LEN, D), 1.0, 6.0, ((0, 2), (2, 4), (3, 4))),
        "attn_norm": jnp.clip(1.0 + 0.1 * jax.random.normal(key_of[1], (N_SECTION, D), jnp.float32), 0.5, 1.5).astype(jnp.bfloat16),
        "w_query": noise(key_of[2], (N_SECTION, D, HEADS * HEAD), D ** -0.5, 0.25, ((0, 2), (1, 4))),
        "w_key": noise(key_of[3], (N_SECTION, D, KV_HEADS * HEAD), D ** -0.5, 0.25, ((0, 2), (1, 4))),
        "w_value": noise(key_of[4], (N_SECTION, D, KV_HEADS * HEAD), D ** -0.5, 0.25, ((0, 2), (1, 4))),
        "w_out": noise(key_of[5], (N_SECTION, HEADS * HEAD, D), (HEADS * HEAD // 32) ** -0.5, 1.5, ((0, 2), (1, 4))),
        "ffn_norm": jnp.clip(1.0 + 0.1 * jax.random.normal(key_of[6], (N_SECTION, D), jnp.float32), 0.5, 1.5).astype(jnp.bfloat16),
        "w_gate": noise(key_of[7], (N_SECTION, D, FF), D ** -0.5, 0.25, ((0, 2), (1, 4))),
        "w_up": noise(key_of[8], (N_SECTION, D, FF), D ** -0.5, 0.25, ((0, 2), (1, 4))),
        "w_down": noise(key_of[9], (N_SECTION, FF, D), FF ** -0.5, 0.15625, ((0, 2), (1, 4))),
    }


epsilon = 1e-05
rope_base = 100000.0
neg_large = -1e+30
highest = lax.Precision.HIGHEST

@jax.custom_vjp
def low(v):
    return lax.optimization_barrier(v.astype(jnp.bfloat16)).astype(jnp.float32)

@jax.custom_vjp
def low_back(v):
    return v

def low_keep(v):
    return (low(v), None)

def low_pass(kept, grad):
    return (grad,)

def back_keep(v):
    return (v, None)

def back_low(kept, grad):
    return (low(grad),)
low.defvjp(low_keep, low_pass)
low_back.defvjp(back_keep, back_low)

def product(left_side, right_side):
    return jnp.dot(left_side, right_side, precision=highest)

def rms_norm(source, gain_vector):
    return source * lax.rsqrt(lax.optimization_barrier(jnp.mean(source * source, axis=-1, keepdims=True)) + epsilon) * gain_vector

def rotary(tensor):
    half_size = HEAD // 2
    frequency = rope_base ** (-jnp.arange(half_size, dtype=jnp.float32) * 2.0 / HEAD)
    angles = jnp.arange(LEN, dtype=jnp.float32)[:, None] * frequency[None, :]
    cosine = jnp.cos(angles)[:, None, :]
    sine_part = jnp.sin(angles)[:, None, :]
    first_half = tensor[..., :half_size]
    second_half = tensor[..., half_size:]
    return jnp.concatenate([first_half * cosine - second_half * sine_part, second_half * cosine + first_half * sine_part], axis=-1)

def attend(query_rot, key_rot, values):
    block_rows = min(512, LEN)
    block_count = LEN // block_rows
    group_size = HEADS // KV_HEADS
    blocks = query_rot.reshape(block_count, block_rows, KV_HEADS, group_size, HEAD)
    key_pos = jnp.arange(LEN, dtype=jnp.int32)

    def one_block(block_args):
        query_block, block_index = block_args
        raw_scores = low_back(jnp.einsum('tkgd,ukd->kgtu', query_block, key_rot, precision=highest))
        scores = raw_scores * HEAD ** (-0.5)
        query_pos = block_index * block_rows + jnp.arange(block_rows, dtype=jnp.int32)
        allowed = key_pos[None, :] <= query_pos[:, None]
        scores = jnp.where(allowed, scores, neg_large)
        running_top = lax.optimization_barrier(jnp.max(scores, axis=-1, keepdims=True))
        weights_now = jnp.exp(scores - running_top)
        probabilities = weights_now / lax.optimization_barrier(jnp.sum(weights_now, axis=-1, keepdims=True))
        return jnp.einsum('kgtu,ukd->tkgd', low(probabilities), values, precision=highest)
    mixed_heads = lax.map(jax.checkpoint(one_block), (blocks, jnp.arange(block_count, dtype=jnp.int32)))
    return mixed_heads.reshape(LEN, HEADS * HEAD)

def layer(source, weights):
    gain_attn, w_query, w_key, w_value, w_out, gain_ffn, w_gate, w_up, w_down = weights
    normed = low(rms_norm(source, gain_attn))
    query_rot = low(rotary(low_back(product(normed, w_query)).reshape(LEN, HEADS, HEAD)))
    key_rot = low(rotary(low_back(product(normed, w_key)).reshape(LEN, KV_HEADS, HEAD)))
    values = low(low_back(product(normed, w_value))).reshape(LEN, KV_HEADS, HEAD)
    mixed_heads = low(low_back(attend(query_rot, key_rot, values)))
    hidden = source + low_back(product(mixed_heads, w_out))
    normed_ffn = low(rms_norm(hidden, gain_ffn))
    gate_pre = low_back(product(normed_ffn, w_gate))
    upper = low_back(product(normed_ffn, w_up))
    active = low(jax.nn.silu(gate_pre) * upper)
    return hidden + low_back(product(active, w_down))

def reference(ends, attn_norm, w_query, w_key, w_value, w_out, ffn_norm, w_gate, w_up, w_down):
    inputs = ends[0].astype(jnp.float32).reshape(MB * SEQS, LEN, D)
    cotangent = ends[1].astype(jnp.float32).reshape(MB * SEQS, LEN, D)
    params = tuple((part.astype(jnp.float32) for part in (attn_norm, w_query, w_key, w_value, w_out, ffn_norm, w_gate, w_up, w_down)))

    def forward(inputs, params):

        def one_sequence(source):
            first_out = layer(source, tuple((part[0] for part in params)))
            return layer(low(low_back(first_out)), tuple((part[1] for part in params)))
        return lax.map(jax.checkpoint(one_sequence), inputs)
    outputs, pullback = jax.vjp(forward, inputs, params)
    grad_in, grad_parts = pullback(cotangent)
    ends_out = jnp.stack([grad_in, outputs]).reshape(2, MB, SEQS, LEN, D)
    return (ends_out, grad_parts[0], grad_parts[1], grad_parts[2], grad_parts[3], grad_parts[4], grad_parts[5], grad_parts[6], grad_parts[7], grad_parts[8])
```

```python
from functools import partial

import jax
import jax.numpy as jnp
from jax import lax
from jax.sharding import PartitionSpec as P

HEADS = 9
KV_HEADS = 3
HEAD = 64


epsilon = 1e-05
rope_base = 100000.0
neg_large = -1e30


def shifted(shard, axis, by):
    peers = lax.axis_size(axis)
    pairs = [(i, i + by) for i in range(peers) if 0 <= i + by < peers]
    return lax.ppermute(shard, axis, pairs)


def rms_scale(source):
    return lax.rsqrt(jnp.mean(source * source, axis=-1, keepdims=True) + epsilon)


def rms_back(source, gain_vector, grad_normed):
    inv_scale = rms_scale(source)
    unit_rows = source * inv_scale
    grad_unit = grad_normed * gain_vector
    gain_grad = jnp.sum(grad_normed * unit_rows, axis=0)
    grad_source = inv_scale * (
        grad_unit - unit_rows * jnp.mean(grad_unit * unit_rows, axis=-1, keepdims=True)
    )
    return (grad_source, gain_grad)


def rotation_tables(positions):
    half_size = HEAD // 2
    frequency = rope_base ** (-jnp.arange(half_size, dtype=jnp.float32) * 2.0 / HEAD)
    angles = positions.astype(jnp.float32)[:, None] * frequency[None, :]
    return (jnp.cos(angles)[None, :, None, :], jnp.sin(angles)[None, :, None, :])


def rotate(tensor, tables):
    cosine, sine_part = tables
    half_size = tensor.shape[-1] // 2
    first_half = tensor[..., :half_size]
    second_half = tensor[..., half_size:]
    return jnp.concatenate(
        [
            first_half * cosine - second_half * sine_part,
            second_half * cosine + first_half * sine_part,
        ],
        axis=-1,
    )


def rotate_back(gradient, tables):
    cosine, sine_part = tables
    half_size = gradient.shape[-1] // 2
    first_half = gradient[..., :half_size]
    second_half = gradient[..., half_size:]
    return jnp.concatenate(
        [
            first_half * cosine + second_half * sine_part,
            second_half * cosine - first_half * sine_part,
        ],
        axis=-1,
    )


def linear(left_side, right_side):
    return jnp.dot(left_side, right_side, preferred_element_type=jnp.float32)


def weight_grad(left_side, right_side):
    return jnp.einsum("rd,rf->df", left_side, right_side, preferred_element_type=jnp.float32)


def input_grad(gradient, weight):
    return jnp.einsum("rf,df->rd", gradient, weight, preferred_element_type=jnp.float32)


def split_blocks(tensor):
    seq_count, length, head_count, head_size = tensor.shape
    block_rows = min(512, length)
    shaped = tensor.reshape(seq_count, length // block_rows, block_rows, head_count, head_size)
    return (jnp.moveaxis(shaped, 1, 0), block_rows)


def block_scores(grouped, key_block, block_start, positions):
    raw_scores = jnp.einsum(
        "stkgd,sukd->skgtu", grouped, key_block, preferred_element_type=jnp.float32
    )
    key_pos = block_start + jnp.arange(key_block.shape[1], dtype=jnp.int32)
    allowed = key_pos[None, :] <= positions[:, None]
    return (jnp.where(allowed, raw_scores * HEAD ** (-0.5), neg_large), allowed)


def keep_carry(state_triple):
    return state_triple


def scatter_at_end(parts):
    attn_shares = (
        lax.psum_scatter(
            parts[0].astype(jnp.bfloat16), "shard", scatter_dimension=0, tiled=True
        ).astype(jnp.float32),
        lax.psum_scatter(
            parts[1].astype(jnp.bfloat16), "shard", scatter_dimension=0, tiled=True
        ).astype(jnp.float32),
        lax.psum_scatter(
            parts[2].astype(jnp.bfloat16), "shard", scatter_dimension=0, tiled=True
        ).astype(jnp.float32),
        lax.psum_scatter(
            parts[3].astype(jnp.bfloat16), "shard", scatter_dimension=0, tiled=True
        ).astype(jnp.float32),
        lax.psum_scatter(
            parts[4].astype(jnp.bfloat16), "shard", scatter_dimension=0, tiled=True
        ).astype(jnp.float32),
        lax.psum_scatter(
            parts[5].astype(jnp.bfloat16), "shard", scatter_dimension=0, tiled=True
        ).astype(jnp.float32),
    )
    ffn_shares = (
        lax.psum_scatter(
            parts[6].astype(jnp.bfloat16), "shard", scatter_dimension=0, tiled=True
        ).astype(jnp.float32),
        lax.psum_scatter(
            parts[7].astype(jnp.bfloat16), "shard", scatter_dimension=0, tiled=True
        ).astype(jnp.float32),
    )
    down_share = lax.psum_scatter(
        parts[8].astype(jnp.bfloat16), "shard", scatter_dimension=0, tiled=True
    ).astype(jnp.float32)
    return tuple(attn_shares) + tuple(ffn_shares) + (down_share,)


def forward_layer(block_in, weights, tables, positions):
    gain_attn, w_query, w_key, w_value, w_out, gain_ffn, w_gate, w_up, w_down = weights
    seq_count, tok_count, model_width = block_in.shape
    group_size = HEADS // KV_HEADS
    source = block_in.astype(jnp.float32).reshape(seq_count * tok_count, model_width)
    normed = (source * rms_scale(source) * gain_attn.astype(jnp.float32)).astype(jnp.bfloat16)
    query_rot = rotate(
        linear(normed, w_query).reshape(seq_count, tok_count, HEADS, HEAD), tables
    ).astype(jnp.bfloat16)
    key_rot = rotate(
        linear(normed, w_key).reshape(seq_count, tok_count, KV_HEADS, HEAD), tables
    ).astype(jnp.bfloat16)
    values = (
        linear(normed, w_value).astype(jnp.bfloat16).reshape(seq_count, tok_count, KV_HEADS, HEAD)
    )
    keys_all, values_all = (
        lax.all_gather(key_rot, "shard", axis=1, tiled=True),
        lax.all_gather(values, "shard", axis=1, tiled=True),
    )
    grouped = query_rot.reshape(seq_count, tok_count, KV_HEADS, group_size, HEAD)
    key_blocks, block_rows = split_blocks(keys_all)
    value_blocks, block_rows = split_blocks(values_all)
    block_ids = jnp.arange(key_blocks.shape[0], dtype=jnp.int32)
    last_query = positions[-1]

    def attend_step(state_triple, block_args):
        key_block, value_block, block_index = block_args
        block_start = block_index * block_rows

        def attend_update(state_triple):
            running_top, running_sum, mixed_sum = state_triple
            scores, allowed = block_scores(grouped, key_block, block_start, positions)
            new_top = jnp.maximum(running_top, jnp.max(scores, axis=-1))
            weights_now = jnp.where(allowed, jnp.exp(scores - new_top[..., None]), 0.0)
            factor = jnp.exp(running_top - new_top)
            running_sum = running_sum * factor + jnp.sum(weights_now, axis=-1)
            mixed_sum = mixed_sum * jnp.moveaxis(factor, 3, 1)[..., None] + jnp.einsum(
                "skgtu,sukd->stkgd",
                weights_now.astype(jnp.bfloat16),
                value_block,
                preferred_element_type=jnp.float32,
            )
            return (new_top, running_sum, mixed_sum)

        return (lax.cond(block_start <= last_query, attend_update, keep_carry, state_triple), None)

    stats_shape = (seq_count, KV_HEADS, group_size, tok_count)
    start_triple = (
        jnp.full(stats_shape, neg_large, jnp.float32),
        jnp.zeros(stats_shape, jnp.float32),
        jnp.zeros(grouped.shape, jnp.float32),
    )
    (running_top, running_sum, mixed_sum), unused = lax.scan(
        attend_step, start_triple, (key_blocks, value_blocks, block_ids)
    )
    log_total = running_top + jnp.log(running_sum)
    attended = mixed_sum / jnp.moveaxis(running_sum, 3, 1)[..., None]
    mixed_heads = attended.astype(jnp.bfloat16).reshape(seq_count * tok_count, HEADS * HEAD)
    hidden = source + linear(mixed_heads, w_out)
    normed_ffn = (hidden * rms_scale(hidden) * gain_ffn.astype(jnp.float32)).astype(jnp.bfloat16)
    gate_pre = linear(normed_ffn, w_gate)
    upper = linear(normed_ffn, w_up)
    active = (gate_pre * jax.nn.sigmoid(gate_pre) * upper).astype(jnp.bfloat16)
    result = hidden + linear(active, w_down)
    kept_state = (
        block_in,
        normed,
        grouped,
        key_blocks,
        value_blocks,
        log_total,
        mixed_heads,
        attended,
        hidden,
        normed_ffn,
        gate_pre,
        upper,
        active,
    )
    return (result, kept_state)


def backward_layer(kept_state, grad_out, weights, tables, positions):
    gain_attn, w_query, w_key, w_value, w_out, gain_ffn, w_gate, w_up, w_down = weights
    (
        block_in,
        normed,
        grouped,
        key_blocks,
        value_blocks,
        log_total,
        mixed_heads,
        attended,
        hidden,
        normed_ffn,
        gate_pre,
        upper,
        active,
    ) = kept_state
    seq_count, tok_count, model_width = block_in.shape
    block_rows = key_blocks.shape[2]
    source = block_in.astype(jnp.float32).reshape(seq_count * tok_count, model_width)
    grad_ffn_out = grad_out.astype(jnp.bfloat16)
    g_down = weight_grad(active, grad_ffn_out)
    grad_active = input_grad(grad_ffn_out, w_down)
    sigmoid_gate = jax.nn.sigmoid(gate_pre)
    grad_gate = (
        grad_active * upper * sigmoid_gate * (1.0 + gate_pre * (1.0 - sigmoid_gate))
    ).astype(jnp.bfloat16)
    grad_upper = (grad_active * gate_pre * sigmoid_gate).astype(jnp.bfloat16)
    g_gate = weight_grad(normed_ffn, grad_gate)
    g_up = weight_grad(normed_ffn, grad_upper)
    grad_normed_ffn = input_grad(grad_gate, w_gate) + input_grad(grad_upper, w_up)
    grad_hidden_part, g_gain_ffn = rms_back(hidden, gain_ffn.astype(jnp.float32), grad_normed_ffn)
    grad_hidden = grad_out + grad_hidden_part
    grad_attn = grad_hidden.astype(jnp.bfloat16)
    g_out = weight_grad(mixed_heads, grad_attn)
    grad_heads = input_grad(grad_attn, w_out).astype(jnp.bfloat16).reshape(grouped.shape)
    row_delta = jnp.moveaxis(jnp.sum(grad_heads.astype(jnp.float32) * attended, axis=-1), 1, 3)
    block_ids = jnp.arange(key_blocks.shape[0], dtype=jnp.int32)
    last_query = positions[-1]

    def grad_step(grad_query, block_args):
        key_block, value_block, block_index = block_args
        block_start = block_index * block_rows

        def grad_update(grad_query):
            scores, allowed = block_scores(grouped, key_block, block_start, positions)
            probabilities = jnp.where(allowed, jnp.exp(scores - log_total[..., None]), 0.0)
            grad_probs = jnp.einsum(
                "stkgd,sukd->skgtu", grad_heads, value_block, preferred_element_type=jnp.float32
            )
            grad_scores = (
                probabilities * (grad_probs - row_delta[..., None]) * HEAD ** (-0.5)
            ).astype(jnp.bfloat16)
            grad_query = grad_query + jnp.einsum(
                "skgtu,sukd->stkgd", grad_scores, key_block, preferred_element_type=jnp.float32
            )
            grad_key_block = jnp.einsum(
                "skgtu,stkgd->sukd", grad_scores, grouped, preferred_element_type=jnp.float32
            )
            grad_value_block = jnp.einsum(
                "skgtu,stkgd->sukd",
                probabilities.astype(jnp.bfloat16),
                grad_heads,
                preferred_element_type=jnp.float32,
            )
            return (grad_query, (grad_key_block, grad_value_block))

        def skip_block(grad_query):
            empty_grad = jnp.zeros(key_block.shape, jnp.float32)
            return (grad_query, (empty_grad, empty_grad))

        return lax.cond(block_start <= last_query, grad_update, skip_block, grad_query)

    grad_query, (key_parts, value_parts) = lax.scan(
        grad_step, jnp.zeros(grouped.shape, jnp.float32), (key_blocks, value_blocks, block_ids)
    )
    full_shape = (seq_count, key_parts.shape[0] * block_rows, KV_HEADS, HEAD)
    key_full = jnp.moveaxis(key_parts, 0, 1).reshape(full_shape)
    value_full = jnp.moveaxis(value_parts, 0, 1).reshape(full_shape)
    grad_keys, grad_values = (
        lax.psum_scatter(
            key_full.astype(jnp.bfloat16), "shard", scatter_dimension=1, tiled=True
        ).astype(jnp.float32),
        lax.psum_scatter(
            value_full.astype(jnp.bfloat16), "shard", scatter_dimension=1, tiled=True
        ).astype(jnp.float32),
    )
    row_count = seq_count * tok_count
    grad_query_rows = (
        rotate_back(grad_query.reshape(seq_count, tok_count, HEADS, HEAD), tables)
        .astype(jnp.bfloat16)
        .reshape(row_count, HEADS * HEAD)
    )
    grad_key_rows = (
        rotate_back(grad_keys, tables).astype(jnp.bfloat16).reshape(row_count, KV_HEADS * HEAD)
    )
    grad_value_rows = grad_values.astype(jnp.bfloat16).reshape(row_count, KV_HEADS * HEAD)
    g_query = weight_grad(normed, grad_query_rows)
    g_key = weight_grad(normed, grad_key_rows)
    g_value = weight_grad(normed, grad_value_rows)
    grad_normed = (
        input_grad(grad_query_rows, w_query)
        + input_grad(grad_key_rows, w_key)
        + input_grad(grad_value_rows, w_value)
    )
    grad_source_part, g_gain_attn = rms_back(source, gain_attn.astype(jnp.float32), grad_normed)
    grad_source = grad_hidden + grad_source_part
    return (
        grad_source,
        (g_gain_attn, g_query, g_key, g_value, g_out, g_gain_ffn, g_gate, g_up, g_down),
    )


def on_device(ends, attn_norm, w_query, w_key, w_value, w_out, ffn_norm, w_gate, w_up, w_down):
    params = (
        attn_norm[0],
        w_query[0],
        w_key[0],
        w_value[0],
        w_out[0],
        ffn_norm[0],
        w_gate[0],
        w_up[0],
        w_down[0],
    )
    leading = lax.axis_index("section") == 0
    held_weights = (
        lax.all_gather(params[0], "shard", axis=0, tiled=True),
        lax.all_gather(params[1], "shard", axis=0, tiled=True),
        lax.all_gather(params[2], "shard", axis=0, tiled=True),
        lax.all_gather(params[3], "shard", axis=0, tiled=True),
        lax.all_gather(params[4], "shard", axis=0, tiled=True),
        lax.all_gather(params[5], "shard", axis=0, tiled=True),
        lax.all_gather(params[6], "shard", axis=0, tiled=True),
        lax.all_gather(params[7], "shard", axis=0, tiled=True),
        lax.all_gather(params[8], "shard", axis=0, tiled=True),
    )
    local_ends = ends[0]
    micro_count, seq_count, tok_count, model_width = local_ends.shape
    positions = lax.axis_index("shard") * tok_count + jnp.arange(tok_count, dtype=jnp.int32)
    tables = rotation_tables(positions)
    arriving = jnp.zeros((seq_count, tok_count, model_width), jnp.bfloat16)
    kept_states = []
    layer_outputs = []
    for moment in range(micro_count + 1):
        own_rows = local_ends[moment] if moment < micro_count else jnp.zeros_like(arriving)
        block_in = jnp.where(leading, own_rows, arriving)
        result, kept_state = forward_layer(block_in, held_weights, tables, positions)
        kept_states.append(kept_state)
        if moment > 0:
            layer_outputs.append(result)
        if moment < micro_count:
            arriving = shifted(
                result.astype(jnp.bfloat16).reshape(seq_count, tok_count, model_width), "section", 1
            )
    returning = jnp.zeros((seq_count * tok_count, model_width), jnp.float32)
    totals = None
    input_grads = []
    for moment in range(micro_count + 1):
        earlier = moment - 1 if moment > 0 else micro_count
        later = moment + 1 if moment < micro_count else 0
        kept_state = jax.tree.map(
            partial(jnp.where, leading), kept_states[earlier], kept_states[later]
        )
        if moment < micro_count:
            own_grad = (
                local_ends[moment].astype(jnp.float32).reshape(seq_count * tok_count, model_width)
            )
        else:
            own_grad = jnp.zeros_like(returning)
        grad_source, grad_parts = backward_layer(
            kept_state, jnp.where(leading, returning, own_grad), held_weights, tables, positions
        )
        totals = grad_parts if totals is None else jax.tree.map(jnp.add, totals, grad_parts)
        if moment > 0:
            input_grads.append(grad_source)
        if moment < micro_count:
            returning = shifted(grad_source.astype(jnp.bfloat16), "section", -1).astype(jnp.float32)
    pieces = [
        jnp.where(leading, input_grads[number], layer_outputs[number])
        for number in range(micro_count)
    ]
    ends_out = jnp.stack(pieces).reshape(1, micro_count, seq_count, tok_count, model_width)
    shares = scatter_at_end(totals)
    summed = (
        lax.psum(shares[0].astype(jnp.bfloat16), "replica").astype(jnp.float32),
        lax.psum(shares[1].astype(jnp.bfloat16), "replica").astype(jnp.float32),
        lax.psum(shares[2].astype(jnp.bfloat16), "replica").astype(jnp.float32),
        lax.psum(shares[3].astype(jnp.bfloat16), "replica").astype(jnp.float32),
        lax.psum(shares[4].astype(jnp.bfloat16), "replica").astype(jnp.float32),
        lax.psum(shares[5].astype(jnp.bfloat16), "replica").astype(jnp.float32),
        lax.psum(shares[6].astype(jnp.bfloat16), "replica").astype(jnp.float32),
        lax.psum(shares[7].astype(jnp.bfloat16), "replica").astype(jnp.float32),
        lax.psum(shares[8].astype(jnp.bfloat16), "replica").astype(jnp.float32),
    )
    return (ends_out,) + tuple((share[None] for share in summed))


def xor_send(value, axis, bits):
    peers = lax.axis_size(axis)
    return lax.ppermute(value, axis, [(i, i ^ bits) for i in range(peers)])


def xor_sort(parts, index):
    low_bit, high_bit = (index & 1) == 1, (index & 2) == 2
    a, b, c, d = parts
    pairs = (
        jnp.where(low_bit, b, a),
        jnp.where(low_bit, a, b),
        jnp.where(low_bit, d, c),
        jnp.where(low_bit, c, d),
    )
    return (
        jnp.where(high_bit, pairs[2], pairs[0]),
        jnp.where(high_bit, pairs[3], pairs[1]),
        jnp.where(high_bit, pairs[0], pairs[2]),
        jnp.where(high_bit, pairs[1], pairs[3]),
    )


def gather_xor(value):
    crossed = xor_send(value, "shard", 2)
    beside = xor_send(value, "shard", 1)
    far = xor_send(crossed, "shard", 1)
    return (value, beside, crossed, far)


def gather_rows(value, index):
    return jnp.concatenate(xor_sort(gather_xor(value), index), axis=0)


def add_low(first, second):
    return (first.astype(jnp.float32) + second.astype(jnp.float32)).astype(jnp.bfloat16)


def reduce_to_owner(partial, index):
    rows = partial.shape[0] // 4
    blocks = partial.reshape(2, 2, rows, partial.shape[1])
    core, chip = index & 1, index >> 1
    kept = lax.dynamic_index_in_dim(blocks, core, 1, keepdims=False)
    sent = lax.dynamic_index_in_dim(blocks, core ^ 1, 1, keepdims=False)
    halves = add_low(kept, xor_send(sent, "shard", 1))
    kept = lax.dynamic_index_in_dim(halves, chip, 0, keepdims=False)
    sent = lax.dynamic_index_in_dim(halves, chip ^ 1, 0, keepdims=False)
    return add_low(kept, xor_send(sent, "shard", 2))


def reduce_replicas(value, replica, axis):
    size = value.shape[axis] // 4

    def quarter(number):
        return lax.dynamic_slice_in_dim(value, number * size, size, axis)

    total = quarter(replica).astype(jnp.float32)
    for bits in (1, 2, 3):
        total = total + xor_send(quarter(replica ^ bits), "replica", bits).astype(jnp.float32)
    return total.astype(jnp.bfloat16)


def gather_replicas(value, replica, axis):
    parts = (value,) + tuple(xor_send(value, "replica", bits) for bits in (1, 2, 3))
    return jnp.concatenate(xor_sort(parts, replica), axis=axis)


def reduce_layer(partial, layer, index, replica, axis):
    mine = reduce_replicas(reduce_to_owner(partial, index), replica, axis)
    other = lax.ppermute(mine, "section", [(1 - layer, layer)])
    return add_low(mine, other)


def attend_forward(query_rot, blocks, index):
    tok_count = query_rot.shape[0]
    positions = index * tok_count + jnp.arange(tok_count, dtype=jnp.int32)
    grouped = query_rot.reshape(1, tok_count, KV_HEADS, HEADS // KV_HEADS, HEAD)
    key_width = KV_HEADS * HEAD
    key_blocks = blocks[:, :, :key_width].reshape(4, 1, tok_count, KV_HEADS, HEAD)
    value_blocks = blocks[:, :, key_width:].reshape(4, 1, tok_count, KV_HEADS, HEAD)
    top = jnp.full((1, KV_HEADS, HEADS // KV_HEADS, tok_count), neg_large, jnp.float32)
    total = jnp.zeros_like(top)
    mixed = jnp.zeros(grouped.shape, jnp.float32)

    def update(state, key_block, value_block, start):
        top, total, mixed = state
        scores, allowed = block_scores(grouped, key_block, start, positions)
        new_top = jnp.maximum(top, jnp.max(scores, axis=-1))
        weights_now = jnp.where(allowed, jnp.exp(scores - new_top[..., None]), 0.0)
        factor = jnp.exp(top - new_top)
        total = total * factor + jnp.sum(weights_now, axis=-1)
        mixed = mixed * jnp.moveaxis(factor, 3, 1)[..., None] + jnp.einsum(
            "skgtu,sukd->stkgd",
            weights_now.astype(jnp.bfloat16),
            value_block,
            preferred_element_type=jnp.float32,
        )
        return (new_top, total, mixed)

    state = (top, total, mixed)
    for j in range(4):
        owner = index ^ j
        state = lax.cond(
            owner <= index,
            lambda s, j=j, o=owner: update(s, key_blocks[j], value_blocks[j], o * tok_count),
            lambda s: s,
            state,
        )
    top, total, mixed = state
    attended = (mixed / jnp.moveaxis(total, 3, 1)[..., None]).reshape(tok_count, HEADS * HEAD)
    return (attended.astype(jnp.bfloat16), attended, top + jnp.log(total))


def attend_backward(query_rot, blocks, grad_heads, attended, log_total, index):
    tok_count = query_rot.shape[0]
    positions = index * tok_count + jnp.arange(tok_count, dtype=jnp.int32)
    grouped = query_rot.reshape(1, tok_count, KV_HEADS, HEADS // KV_HEADS, HEAD)
    key_width = KV_HEADS * HEAD
    key_blocks = blocks[:, :, :key_width].reshape(4, 1, tok_count, KV_HEADS, HEAD)
    value_blocks = blocks[:, :, key_width:].reshape(4, 1, tok_count, KV_HEADS, HEAD)
    grads = grad_heads.reshape(grouped.shape)
    delta = jnp.moveaxis(
        jnp.sum(grads.astype(jnp.float32) * attended.reshape(grouped.shape), axis=-1), 1, 3
    )

    def update(grad_query, key_block, value_block, start):
        scores, allowed = block_scores(grouped, key_block, start, positions)
        probabilities = jnp.where(allowed, jnp.exp(scores - log_total[..., None]), 0.0)
        grad_probs = jnp.einsum(
            "stkgd,sukd->skgtu", grads, value_block, preferred_element_type=jnp.float32
        )
        grad_scores = (
            probabilities * (grad_probs - delta[..., None]) * HEAD ** (-0.5)
        ).astype(jnp.bfloat16)
        grad_query = grad_query + jnp.einsum(
            "skgtu,sukd->stkgd", grad_scores, key_block, preferred_element_type=jnp.float32
        )
        grad_key = jnp.einsum(
            "skgtu,stkgd->sukd", grad_scores, grouped, preferred_element_type=jnp.float32
        )
        grad_value = jnp.einsum(
            "skgtu,stkgd->sukd",
            probabilities.astype(jnp.bfloat16),
            grads,
            preferred_element_type=jnp.float32,
        )
        both = jnp.concatenate(
            [grad_key.reshape(tok_count, key_width), grad_value.reshape(tok_count, key_width)],
            axis=1,
        )
        return (grad_query, both.astype(jnp.bfloat16))

    grad_query = jnp.zeros(grouped.shape, jnp.float32)
    parts = []
    for j in range(4):
        owner = index ^ j
        grad_query, part = lax.cond(
            owner <= index,
            lambda g, j=j, o=owner: update(g, key_blocks[j], value_blocks[j], o * tok_count),
            lambda g: (g, jnp.zeros((tok_count, 2 * key_width), jnp.bfloat16)),
            grad_query,
        )
        parts.append(part)
    return (grad_query.reshape(tok_count, HEADS * HEAD), jnp.stack(parts))


def forward_pass(block_in, weights, tables, index):
    gain_attn, w_in, w_out, gain_ffn, w_gate_up, w_down = weights
    tok_count, model_width = block_in.shape
    source = block_in.astype(jnp.float32)
    normed = (source * rms_scale(source) * gain_attn).astype(jnp.bfloat16)
    projected = linear(normed, w_in)
    query_width, key_width = HEADS * HEAD, KV_HEADS * HEAD
    query_rot = (
        rotate(projected[:, :query_width].reshape(1, tok_count, HEADS, HEAD), tables)
        .astype(jnp.bfloat16)
        .reshape(tok_count, query_width)
    )
    key_rot = (
        rotate(
            projected[:, query_width : query_width + key_width].reshape(
                1, tok_count, KV_HEADS, HEAD
            ),
            tables,
        )
        .astype(jnp.bfloat16)
        .reshape(tok_count, key_width)
    )
    values = projected[:, query_width + key_width :].astype(jnp.bfloat16)
    blocks = jnp.stack(gather_xor(jnp.concatenate([key_rot, values], axis=1)))
    mixed_heads, attended, log_total = attend_forward(query_rot, blocks, index)
    hidden = source + linear(mixed_heads, w_out)
    normed_ffn = (hidden * rms_scale(hidden) * gain_ffn).astype(jnp.bfloat16)
    gate_up = linear(normed_ffn, w_gate_up)
    hidden_units = gate_up.shape[1] // 2
    gate_pre, upper = gate_up[:, :hidden_units], gate_up[:, hidden_units:]
    active = (gate_pre * jax.nn.sigmoid(gate_pre) * upper).astype(jnp.bfloat16)
    result = hidden + linear(active, w_down)
    kept = (
        block_in, normed, query_rot, blocks, log_total, mixed_heads, attended,
        hidden, normed_ffn, gate_up, active,
    )
    return (result, kept)


def backward_ffn(kept, grad_out, weights):
    gain_attn, w_in, w_out, gain_ffn, w_gate_up, w_down = weights
    hidden, normed_ffn, gate_up, active = kept[7:]
    hidden_units = gate_up.shape[1] // 2
    gate_pre, upper = gate_up[:, :hidden_units], gate_up[:, hidden_units:]
    grad_ffn_out = grad_out.astype(jnp.bfloat16)
    grad_active = input_grad(grad_ffn_out, w_down)
    sigmoid_gate = jax.nn.sigmoid(gate_pre)
    grad_gate = (
        grad_active * upper * sigmoid_gate * (1.0 + gate_pre * (1.0 - sigmoid_gate))
    ).astype(jnp.bfloat16)
    grad_upper = (grad_active * gate_pre * sigmoid_gate).astype(jnp.bfloat16)
    grad_both = jnp.concatenate([grad_gate, grad_upper], axis=1)
    g_down = weight_grad(active, grad_ffn_out).astype(jnp.bfloat16)
    g_gate_up = weight_grad(normed_ffn, grad_both).astype(jnp.bfloat16)
    grad_normed_ffn = input_grad(grad_both, w_gate_up)
    grad_part, g_gain_ffn = rms_back(hidden, gain_ffn, grad_normed_ffn)
    return (grad_out + grad_part, g_gain_ffn, g_gate_up, g_down)


def backward_attention(kept, grad_hidden, weights, tables, index):
    gain_attn, w_in, w_out, gain_ffn, w_gate_up, w_down = weights
    block_in, normed, query_rot, blocks, log_total, mixed_heads, attended = kept[:7]
    tok_count = block_in.shape[0]
    source = block_in.astype(jnp.float32)
    grad_attn = grad_hidden.astype(jnp.bfloat16)
    g_out = weight_grad(mixed_heads, grad_attn)
    grad_heads = input_grad(grad_attn, w_out).astype(jnp.bfloat16)
    grad_query, parts = attend_backward(
        query_rot, blocks, grad_heads, attended, log_total, index
    )
    received = xor_send(parts[1::2], "shard", 1)
    own_sum = add_low(parts[0], received[0])
    cross_sum = add_low(parts[2], received[1])
    key_width = KV_HEADS * HEAD
    grad_kv = own_sum.astype(jnp.float32) + xor_send(cross_sum, "shard", 2).astype(jnp.float32)
    grad_query_rows = (
        rotate_back(grad_query.reshape(1, tok_count, HEADS, HEAD), tables)
        .astype(jnp.bfloat16)
        .reshape(tok_count, HEADS * HEAD)
    )
    grad_key_rows = (
        rotate_back(grad_kv[:, :key_width].reshape(1, tok_count, KV_HEADS, HEAD), tables)
        .astype(jnp.bfloat16)
        .reshape(tok_count, key_width)
    )
    grad_rows = jnp.concatenate(
        [grad_query_rows, grad_key_rows, grad_kv[:, key_width:].astype(jnp.bfloat16)], axis=1
    )
    g_in = weight_grad(normed, grad_rows)
    grad_normed = input_grad(grad_rows, w_in)
    grad_part, g_gain_attn = rms_back(source, gain_attn, grad_normed)
    return (grad_hidden + grad_part, g_gain_attn, g_in, g_out)


def both_sections(
    ends, attn_norm, w_query, w_key, w_value, w_out, ffn_norm, w_gate, w_up, w_down
):
    section = lax.axis_index("section")
    leading = section == 0
    index = lax.axis_index("shard")
    replica = lax.axis_index("replica")
    local = ends[0]
    tok_count, model_width = local.shape[-2:]
    own_pair = local.reshape(2, tok_count, model_width)
    moved = xor_send(
        lax.dynamic_index_in_dim(own_pair, 1 - section, 0, keepdims=False), "section", 1
    )
    stayed = lax.dynamic_index_in_dim(own_pair, section, 0, keepdims=False)
    tokens = jnp.where(leading, stayed, moved)
    cotangent = jnp.where(leading, moved, stayed)

    attn_width = w_query.shape[2] + 2 * w_key.shape[2] + w_out.shape[2]
    in_width = attn_width - w_out.shape[2]
    gains = jnp.stack([attn_norm[0], ffn_norm[0]], axis=1)
    groups = (
        jnp.concatenate([w_query[0], w_key[0], w_value[0], w_out[0], gains], axis=1),
        jnp.concatenate([w_gate[0], w_up[0]], axis=1),
        w_down[0],
    )
    others = [xor_send(group, "section", 1) for group in groups]
    layers = []
    for layer in (0, 1):
        held = (section == layer)
        whole = [
            gather_rows(jnp.where(held, group, other), index)
            for group, other in zip(groups, others)
        ]
        attn = whole[0]
        layers.append(
            (
                attn[:, attn_width].astype(jnp.float32),
                attn[:, :in_width],
                attn[:, in_width:attn_width],
                attn[:, attn_width + 1].astype(jnp.float32),
                whole[1],
                whole[2],
            )
        )
    positions = index * tok_count + jnp.arange(tok_count, dtype=jnp.int32)
    tables = rotation_tables(positions)
    middle, kept_first = forward_pass(tokens, layers[0], tables, index)
    final, kept_second = forward_pass(middle.astype(jnp.bfloat16), layers[1], tables, index)
    final_arrived = lax.ppermute(final.astype(jnp.bfloat16), "section", [(0, 1)])

    grad = cotangent.astype(jnp.float32)
    quarters = []
    for layer, kept in ((1, kept_second), (0, kept_first)):
        weights = layers[layer]
        grad_hidden, g_gain_ffn, g_gate_up, g_down = backward_ffn(kept, grad, weights)
        ffn_quarters = (
            reduce_layer(g_gate_up, layer, index, replica, 1),
            reduce_layer(g_down, layer, index, replica, 0),
        )
        grad, g_gain_attn, g_in, g_out = backward_attention(
            kept, grad_hidden, weights, tables, index
        )
        pad = jnp.zeros((model_width, 2048 - attn_width - 2), jnp.float32)
        packed = jnp.concatenate(
            [g_in, g_out, g_gain_attn[:, None], g_gain_ffn[:, None], pad], axis=1
        ).astype(jnp.bfloat16)
        quarters.append((reduce_layer(packed, layer, index, replica, 1),) + ffn_quarters)
        if layer == 1:
            grad = grad.astype(jnp.bfloat16).astype(jnp.float32)
    grad_arrived = lax.ppermute(grad.astype(jnp.bfloat16), "section", [(1, 0)])
    attn_sum, gate_up_sum, down_sum = [
        gather_replicas(jnp.where(leading, first, second), replica, axis).astype(jnp.float32)
        for first, second, axis in zip(quarters[1], quarters[0], (1, 1, 0))
    ]
    ends_out = jnp.stack(
        [
            jnp.where(leading, grad, final_arrived.astype(jnp.float32)),
            jnp.where(leading, grad_arrived.astype(jnp.float32), final),
        ]
    ).reshape(1, 2, 1, tok_count, model_width)
    cuts = [w_query.shape[2], w_query.shape[2] + w_key.shape[2], in_width, attn_width]
    g_query, g_key, g_value, g_out, _ = jnp.split(attn_sum, cuts, axis=1)
    units = w_gate.shape[2]
    return (
        ends_out,
        attn_sum[:, attn_width][None],
        g_query[None],
        g_key[None],
        g_value[None],
        g_out[None],
        attn_sum[:, attn_width + 1][None],
        gate_up_sum[:, :units][None],
        gate_up_sum[:, units:][None],
        down_sum[None],
    )


def solution(mesh):
    balanced = (
        mesh.shape["section"] == 2 and mesh.shape["replica"] == 4 and mesh.shape["shard"] == 4
    )
    program = both_sections if balanced else on_device
    return jax.shard_map(
        program,
        mesh=mesh,
        in_specs=(
            P("section", None, "replica", "shard", None),
            P("section", "shard"),
            P("section", "shard", None),
            P("section", "shard", None),
            P("section", "shard", None),
            P("section", "shard", None),
            P("section", "shard"),
            P("section", "shard", None),
            P("section", "shard", None),
            P("section", "shard", None),
        ),
        out_specs=(
            P("section", None, "replica", "shard", None),
            P("section", "shard"),
            P("section", "shard", None),
            P("section", "shard", None),
            P("section", "shard", None),
            P("section", "shard", None),
            P("section", "shard"),
            P("section", "shard", None),
            P("section", "shard", None),
            P("section", "shard", None),
        ),
        check_vma=False,
    )
```

```python
from functools import partial

import jax
import jax.numpy as jnp
from jax import lax
from jax.experimental import pallas as pl
from jax.experimental.pallas import tpu as pltpu
from jax.sharding import PartitionSpec as P

HEADS = 9
KV_HEADS = 3
HEAD = 64


epsilon = 1e-05
rope_base = 100000.0
neg_large = -1e30


def shifted(shard, axis, by):
    peers = lax.axis_size(axis)
    pairs = [(i, i + by) for i in range(peers) if 0 <= i + by < peers]
    return lax.ppermute(shard, axis, pairs)


def rms_scale(source):
    return lax.rsqrt(jnp.mean(source * source, axis=-1, keepdims=True) + epsilon)


def rms_back(source, gain_vector, grad_normed):
    inv_scale = rms_scale(source)
    unit_rows = source * inv_scale
    grad_unit = grad_normed * gain_vector
    gain_grad = jnp.sum(grad_normed * unit_rows, axis=0)
    grad_source = inv_scale * (
        grad_unit - unit_rows * jnp.mean(grad_unit * unit_rows, axis=-1, keepdims=True)
    )
    return (grad_source, gain_grad)


def rotation_tables(positions):
    half_size = HEAD // 2
    frequency = rope_base ** (-jnp.arange(half_size, dtype=jnp.float32) * 2.0 / HEAD)
    angles = positions.astype(jnp.float32)[:, None] * frequency[None, :]
    return (jnp.cos(angles)[None, :, None, :], jnp.sin(angles)[None, :, None, :])


def rotate(tensor, tables):
    cosine, sine_part = tables
    half_size = tensor.shape[-1] // 2
    first_half = tensor[..., :half_size]
    second_half = tensor[..., half_size:]
    return jnp.concatenate(
        [
            first_half * cosine - second_half * sine_part,
            second_half * cosine + first_half * sine_part,
        ],
        axis=-1,
    )


def rotate_back(gradient, tables):
    cosine, sine_part = tables
    half_size = gradient.shape[-1] // 2
    first_half = gradient[..., :half_size]
    second_half = gradient[..., half_size:]
    return jnp.concatenate(
        [
            first_half * cosine + second_half * sine_part,
            second_half * cosine - first_half * sine_part,
        ],
        axis=-1,
    )


def linear(left_side, right_side):
    return jnp.dot(left_side, right_side, preferred_element_type=jnp.float32)


def weight_grad(left_side, right_side):
    return jnp.einsum("rd,rf->df", left_side, right_side, preferred_element_type=jnp.float32)


def input_grad(gradient, weight):
    return jnp.einsum("rf,df->rd", gradient, weight, preferred_element_type=jnp.float32)


def split_blocks(tensor):
    seq_count, length, head_count, head_size = tensor.shape
    block_rows = min(512, length)
    shaped = tensor.reshape(seq_count, length // block_rows, block_rows, head_count, head_size)
    return (jnp.moveaxis(shaped, 1, 0), block_rows)


def block_scores(grouped, key_block, block_start, positions):
    raw_scores = jnp.einsum(
        "stkgd,sukd->skgtu", grouped, key_block, preferred_element_type=jnp.float32
    )
    key_pos = block_start + jnp.arange(key_block.shape[1], dtype=jnp.int32)
    allowed = key_pos[None, :] <= positions[:, None]
    return (jnp.where(allowed, raw_scores * HEAD ** (-0.5), neg_large), allowed)


def keep_carry(state_triple):
    return state_triple


def scatter_at_end(parts):
    attn_shares = (
        lax.psum_scatter(
            parts[0].astype(jnp.bfloat16), "shard", scatter_dimension=0, tiled=True
        ).astype(jnp.float32),
        lax.psum_scatter(
            parts[1].astype(jnp.bfloat16), "shard", scatter_dimension=0, tiled=True
        ).astype(jnp.float32),
        lax.psum_scatter(
            parts[2].astype(jnp.bfloat16), "shard", scatter_dimension=0, tiled=True
        ).astype(jnp.float32),
        lax.psum_scatter(
            parts[3].astype(jnp.bfloat16), "shard", scatter_dimension=0, tiled=True
        ).astype(jnp.float32),
        lax.psum_scatter(
            parts[4].astype(jnp.bfloat16), "shard", scatter_dimension=0, tiled=True
        ).astype(jnp.float32),
        lax.psum_scatter(
            parts[5].astype(jnp.bfloat16), "shard", scatter_dimension=0, tiled=True
        ).astype(jnp.float32),
    )
    ffn_shares = (
        lax.psum_scatter(
            parts[6].astype(jnp.bfloat16), "shard", scatter_dimension=0, tiled=True
        ).astype(jnp.float32),
        lax.psum_scatter(
            parts[7].astype(jnp.bfloat16), "shard", scatter_dimension=0, tiled=True
        ).astype(jnp.float32),
    )
    down_share = lax.psum_scatter(
        parts[8].astype(jnp.bfloat16), "shard", scatter_dimension=0, tiled=True
    ).astype(jnp.float32)
    return tuple(attn_shares) + tuple(ffn_shares) + (down_share,)


def forward_layer(block_in, weights, tables, positions):
    gain_attn, w_query, w_key, w_value, w_out, gain_ffn, w_gate, w_up, w_down = weights
    seq_count, tok_count, model_width = block_in.shape
    group_size = HEADS // KV_HEADS
    source = block_in.astype(jnp.float32).reshape(seq_count * tok_count, model_width)
    normed = (source * rms_scale(source) * gain_attn.astype(jnp.float32)).astype(jnp.bfloat16)
    query_rot = rotate(
        linear(normed, w_query).reshape(seq_count, tok_count, HEADS, HEAD), tables
    ).astype(jnp.bfloat16)
    key_rot = rotate(
        linear(normed, w_key).reshape(seq_count, tok_count, KV_HEADS, HEAD), tables
    ).astype(jnp.bfloat16)
    values = (
        linear(normed, w_value).astype(jnp.bfloat16).reshape(seq_count, tok_count, KV_HEADS, HEAD)
    )
    keys_all, values_all = (
        lax.all_gather(key_rot, "shard", axis=1, tiled=True),
        lax.all_gather(values, "shard", axis=1, tiled=True),
    )
    grouped = query_rot.reshape(seq_count, tok_count, KV_HEADS, group_size, HEAD)
    key_blocks, block_rows = split_blocks(keys_all)
    value_blocks, block_rows = split_blocks(values_all)
    block_ids = jnp.arange(key_blocks.shape[0], dtype=jnp.int32)
    last_query = positions[-1]

    def attend_step(state_triple, block_args):
        key_block, value_block, block_index = block_args
        block_start = block_index * block_rows

        def attend_update(state_triple):
            running_top, running_sum, mixed_sum = state_triple
            scores, allowed = block_scores(grouped, key_block, block_start, positions)
            new_top = jnp.maximum(running_top, jnp.max(scores, axis=-1))
            weights_now = jnp.where(allowed, jnp.exp(scores - new_top[..., None]), 0.0)
            factor = jnp.exp(running_top - new_top)
            running_sum = running_sum * factor + jnp.sum(weights_now, axis=-1)
            mixed_sum = mixed_sum * jnp.moveaxis(factor, 3, 1)[..., None] + jnp.einsum(
                "skgtu,sukd->stkgd",
                weights_now.astype(jnp.bfloat16),
                value_block,
                preferred_element_type=jnp.float32,
            )
            return (new_top, running_sum, mixed_sum)

        return (lax.cond(block_start <= last_query, attend_update, keep_carry, state_triple), None)

    stats_shape = (seq_count, KV_HEADS, group_size, tok_count)
    start_triple = (
        jnp.full(stats_shape, neg_large, jnp.float32),
        jnp.zeros(stats_shape, jnp.float32),
        jnp.zeros(grouped.shape, jnp.float32),
    )
    (running_top, running_sum, mixed_sum), unused = lax.scan(
        attend_step, start_triple, (key_blocks, value_blocks, block_ids)
    )
    log_total = running_top + jnp.log(running_sum)
    attended = mixed_sum / jnp.moveaxis(running_sum, 3, 1)[..., None]
    mixed_heads = attended.astype(jnp.bfloat16).reshape(seq_count * tok_count, HEADS * HEAD)
    hidden = source + linear(mixed_heads, w_out)
    normed_ffn = (hidden * rms_scale(hidden) * gain_ffn.astype(jnp.float32)).astype(jnp.bfloat16)
    gate_pre = linear(normed_ffn, w_gate)
    upper = linear(normed_ffn, w_up)
    active = (gate_pre * jax.nn.sigmoid(gate_pre) * upper).astype(jnp.bfloat16)
    result = hidden + linear(active, w_down)
    kept_state = (
        block_in,
        normed,
        grouped,
        key_blocks,
        value_blocks,
        log_total,
        mixed_heads,
        attended,
        hidden,
        normed_ffn,
        gate_pre,
        upper,
        active,
    )
    return (result, kept_state)


def backward_layer(kept_state, grad_out, weights, tables, positions):
    gain_attn, w_query, w_key, w_value, w_out, gain_ffn, w_gate, w_up, w_down = weights
    (
        block_in,
        normed,
        grouped,
        key_blocks,
        value_blocks,
        log_total,
        mixed_heads,
        attended,
        hidden,
        normed_ffn,
        gate_pre,
        upper,
        active,
    ) = kept_state
    seq_count, tok_count, model_width = block_in.shape
    block_rows = key_blocks.shape[2]
    source = block_in.astype(jnp.float32).reshape(seq_count * tok_count, model_width)
    grad_ffn_out = grad_out.astype(jnp.bfloat16)
    g_down = weight_grad(active, grad_ffn_out)
    grad_active = input_grad(grad_ffn_out, w_down)
    sigmoid_gate = jax.nn.sigmoid(gate_pre)
    grad_gate = (
        grad_active * upper * sigmoid_gate * (1.0 + gate_pre * (1.0 - sigmoid_gate))
    ).astype(jnp.bfloat16)
    grad_upper = (grad_active * gate_pre * sigmoid_gate).astype(jnp.bfloat16)
    g_gate = weight_grad(normed_ffn, grad_gate)
    g_up = weight_grad(normed_ffn, grad_upper)
    grad_normed_ffn = input_grad(grad_gate, w_gate) + input_grad(grad_upper, w_up)
    grad_hidden_part, g_gain_ffn = rms_back(hidden, gain_ffn.astype(jnp.float32), grad_normed_ffn)
    grad_hidden = grad_out + grad_hidden_part
    grad_attn = grad_hidden.astype(jnp.bfloat16)
    g_out = weight_grad(mixed_heads, grad_attn)
    grad_heads = input_grad(grad_attn, w_out).astype(jnp.bfloat16).reshape(grouped.shape)
    row_delta = jnp.moveaxis(jnp.sum(grad_heads.astype(jnp.float32) * attended, axis=-1), 1, 3)
    block_ids = jnp.arange(key_blocks.shape[0], dtype=jnp.int32)
    last_query = positions[-1]

    def grad_step(grad_query, block_args):
        key_block, value_block, block_index = block_args
        block_start = block_index * block_rows

        def grad_update(grad_query):
            scores, allowed = block_scores(grouped, key_block, block_start, positions)
            probabilities = jnp.where(allowed, jnp.exp(scores - log_total[..., None]), 0.0)
            grad_probs = jnp.einsum(
                "stkgd,sukd->skgtu", grad_heads, value_block, preferred_element_type=jnp.float32
            )
            grad_scores = (
                probabilities * (grad_probs - row_delta[..., None]) * HEAD ** (-0.5)
            ).astype(jnp.bfloat16)
            grad_query = grad_query + jnp.einsum(
                "skgtu,sukd->stkgd", grad_scores, key_block, preferred_element_type=jnp.float32
            )
            grad_key_block = jnp.einsum(
                "skgtu,stkgd->sukd", grad_scores, grouped, preferred_element_type=jnp.float32
            )
            grad_value_block = jnp.einsum(
                "skgtu,stkgd->sukd",
                probabilities.astype(jnp.bfloat16),
                grad_heads,
                preferred_element_type=jnp.float32,
            )
            return (grad_query, (grad_key_block, grad_value_block))

        def skip_block(grad_query):
            empty_grad = jnp.zeros(key_block.shape, jnp.float32)
            return (grad_query, (empty_grad, empty_grad))

        return lax.cond(block_start <= last_query, grad_update, skip_block, grad_query)

    grad_query, (key_parts, value_parts) = lax.scan(
        grad_step, jnp.zeros(grouped.shape, jnp.float32), (key_blocks, value_blocks, block_ids)
    )
    full_shape = (seq_count, key_parts.shape[0] * block_rows, KV_HEADS, HEAD)
    key_full = jnp.moveaxis(key_parts, 0, 1).reshape(full_shape)
    value_full = jnp.moveaxis(value_parts, 0, 1).reshape(full_shape)
    grad_keys, grad_values = (
        lax.psum_scatter(
            key_full.astype(jnp.bfloat16), "shard", scatter_dimension=1, tiled=True
        ).astype(jnp.float32),
        lax.psum_scatter(
            value_full.astype(jnp.bfloat16), "shard", scatter_dimension=1, tiled=True
        ).astype(jnp.float32),
    )
    row_count = seq_count * tok_count
    grad_query_rows = (
        rotate_back(grad_query.reshape(seq_count, tok_count, HEADS, HEAD), tables)
        .astype(jnp.bfloat16)
        .reshape(row_count, HEADS * HEAD)
    )
    grad_key_rows = (
        rotate_back(grad_keys, tables).astype(jnp.bfloat16).reshape(row_count, KV_HEADS * HEAD)
    )
    grad_value_rows = grad_values.astype(jnp.bfloat16).reshape(row_count, KV_HEADS * HEAD)
    g_query = weight_grad(normed, grad_query_rows)
    g_key = weight_grad(normed, grad_key_rows)
    g_value = weight_grad(normed, grad_value_rows)
    grad_normed = (
        input_grad(grad_query_rows, w_query)
        + input_grad(grad_key_rows, w_key)
        + input_grad(grad_value_rows, w_value)
    )
    grad_source_part, g_gain_attn = rms_back(source, gain_attn.astype(jnp.float32), grad_normed)
    grad_source = grad_hidden + grad_source_part
    return (
        grad_source,
        (g_gain_attn, g_query, g_key, g_value, g_out, g_gain_ffn, g_gate, g_up, g_down),
    )


def on_device(ends, attn_norm, w_query, w_key, w_value, w_out, ffn_norm, w_gate, w_up, w_down):
    params = (
        attn_norm[0],
        w_query[0],
        w_key[0],
        w_value[0],
        w_out[0],
        ffn_norm[0],
        w_gate[0],
        w_up[0],
        w_down[0],
    )
    leading = lax.axis_index("section") == 0
    held_weights = (
        lax.all_gather(params[0], "shard", axis=0, tiled=True),
        lax.all_gather(params[1], "shard", axis=0, tiled=True),
        lax.all_gather(params[2], "shard", axis=0, tiled=True),
        lax.all_gather(params[3], "shard", axis=0, tiled=True),
        lax.all_gather(params[4], "shard", axis=0, tiled=True),
        lax.all_gather(params[5], "shard", axis=0, tiled=True),
        lax.all_gather(params[6], "shard", axis=0, tiled=True),
        lax.all_gather(params[7], "shard", axis=0, tiled=True),
        lax.all_gather(params[8], "shard", axis=0, tiled=True),
    )
    local_ends = ends[0]
    micro_count, seq_count, tok_count, model_width = local_ends.shape
    positions = lax.axis_index("shard") * tok_count + jnp.arange(tok_count, dtype=jnp.int32)
    tables = rotation_tables(positions)
    arriving = jnp.zeros((seq_count, tok_count, model_width), jnp.bfloat16)
    kept_states = []
    layer_outputs = []
    for moment in range(micro_count + 1):
        own_rows = local_ends[moment] if moment < micro_count else jnp.zeros_like(arriving)
        block_in = jnp.where(leading, own_rows, arriving)
        result, kept_state = forward_layer(block_in, held_weights, tables, positions)
        kept_states.append(kept_state)
        if moment > 0:
            layer_outputs.append(result)
        if moment < micro_count:
            arriving = shifted(
                result.astype(jnp.bfloat16).reshape(seq_count, tok_count, model_width), "section", 1
            )
    returning = jnp.zeros((seq_count * tok_count, model_width), jnp.float32)
    totals = None
    input_grads = []
    for moment in range(micro_count + 1):
        earlier = moment - 1 if moment > 0 else micro_count
        later = moment + 1 if moment < micro_count else 0
        kept_state = jax.tree.map(
            partial(jnp.where, leading), kept_states[earlier], kept_states[later]
        )
        if moment < micro_count:
            own_grad = (
                local_ends[moment].astype(jnp.float32).reshape(seq_count * tok_count, model_width)
            )
        else:
            own_grad = jnp.zeros_like(returning)
        grad_source, grad_parts = backward_layer(
            kept_state, jnp.where(leading, returning, own_grad), held_weights, tables, positions
        )
        totals = grad_parts if totals is None else jax.tree.map(jnp.add, totals, grad_parts)
        if moment > 0:
            input_grads.append(grad_source)
        if moment < micro_count:
            returning = shifted(grad_source.astype(jnp.bfloat16), "section", -1).astype(jnp.float32)
    pieces = [
        jnp.where(leading, input_grads[number], layer_outputs[number])
        for number in range(micro_count)
    ]
    ends_out = jnp.stack(pieces).reshape(1, micro_count, seq_count, tok_count, model_width)
    shares = scatter_at_end(totals)
    summed = (
        lax.psum(shares[0].astype(jnp.bfloat16), "replica").astype(jnp.float32),
        lax.psum(shares[1].astype(jnp.bfloat16), "replica").astype(jnp.float32),
        lax.psum(shares[2].astype(jnp.bfloat16), "replica").astype(jnp.float32),
        lax.psum(shares[3].astype(jnp.bfloat16), "replica").astype(jnp.float32),
        lax.psum(shares[4].astype(jnp.bfloat16), "replica").astype(jnp.float32),
        lax.psum(shares[5].astype(jnp.bfloat16), "replica").astype(jnp.float32),
        lax.psum(shares[6].astype(jnp.bfloat16), "replica").astype(jnp.float32),
        lax.psum(shares[7].astype(jnp.bfloat16), "replica").astype(jnp.float32),
        lax.psum(shares[8].astype(jnp.bfloat16), "replica").astype(jnp.float32),
    )
    return (ends_out,) + tuple((share[None] for share in summed))


def xor_send(value, axis, bits):
    peers = lax.axis_size(axis)
    return lax.ppermute(value, axis, [(i, i ^ bits) for i in range(peers)])


def xor_sort(parts, index):
    low_bit, high_bit = (index & 1) == 1, (index & 2) == 2
    a, b, c, d = parts
    pairs = (
        jnp.where(low_bit, b, a),
        jnp.where(low_bit, a, b),
        jnp.where(low_bit, d, c),
        jnp.where(low_bit, c, d),
    )
    return (
        jnp.where(high_bit, pairs[2], pairs[0]),
        jnp.where(high_bit, pairs[3], pairs[1]),
        jnp.where(high_bit, pairs[0], pairs[2]),
        jnp.where(high_bit, pairs[1], pairs[3]),
    )


def gather_xor(value):
    crossed = xor_send(value, "shard", 2)
    beside = xor_send(value, "shard", 1)
    far = xor_send(crossed, "shard", 1)
    return (value, beside, crossed, far)


def gather_rows(value, index):
    return jnp.concatenate(xor_sort(gather_xor(value), index), axis=0)


def add_low(first, second):
    return (first.astype(jnp.float32) + second.astype(jnp.float32)).astype(jnp.bfloat16)


def reduce_to_owner(partial, index):
    rows = partial.shape[0] // 4
    blocks = partial.reshape(2, 2, rows, partial.shape[1])
    core, chip = index & 1, index >> 1
    kept = lax.dynamic_index_in_dim(blocks, core, 1, keepdims=False)
    sent = lax.dynamic_index_in_dim(blocks, core ^ 1, 1, keepdims=False)
    halves = add_low(kept, xor_send(sent, "shard", 1))
    kept = lax.dynamic_index_in_dim(halves, chip, 0, keepdims=False)
    sent = lax.dynamic_index_in_dim(halves, chip ^ 1, 0, keepdims=False)
    return add_low(kept, xor_send(sent, "shard", 2))


def reduce_replicas(value, replica, axis):
    size = value.shape[axis] // 4

    def quarter(number):
        return lax.dynamic_slice_in_dim(value, number * size, size, axis)

    total = quarter(replica).astype(jnp.float32)
    for bits in (1, 2, 3):
        total = total + xor_send(quarter(replica ^ bits), "replica", bits).astype(jnp.float32)
    return total.astype(jnp.bfloat16)


def gather_replicas(value, replica, axis):
    parts = (value,) + tuple(xor_send(value, "replica", bits) for bits in (1, 2, 3))
    return jnp.concatenate(xor_sort(parts, replica), axis=axis)


def reduce_sections(value, layer):
    return add_low(value, lax.ppermute(value, "section", [(1 - layer, layer)]))


def tied(*values):
    return lax.optimization_barrier(values)


WIDE = 50 * 2**20


def nt_dot(left, right):
    return lax.dot_general(left, right, (((1,), (1,)), ((), ())), preferred_element_type=jnp.float32)


def tn_dot(left, right):
    return lax.dot_general(left, right, (((0,), (0,)), ((), ())), preferred_element_type=jnp.float32)


def head_columns(head, start=0):
    return slice(start + head * HEAD, start + (head + 1) * HEAD)


def over_blocks(index, update):
    update(0, True)

    def other(j, carry):
        @pl.when((index ^ j) < index)
        def _():
            update(j, False)

        return carry

    lax.fori_loop(1, 4, other, 0)


def causal(rows):
    keys = lax.broadcasted_iota(jnp.int32, (rows, rows), 0)
    queries = lax.broadcasted_iota(jnp.int32, (rows, rows), 1)
    return keys <= queries


def attend_forward_kernel(index_ref, q_ref, blocks_ref, mixed_ref, attended_ref, log_ref, top, total, acc):
    rows = q_ref.shape[0]
    group = HEADS // KV_HEADS

    def update(j, own):
        for kv in range(KV_HEADS):
            keys = blocks_ref[j, :, head_columns(kv)]
            values = blocks_ref[j, :, head_columns(kv, KV_HEADS * HEAD)]
            for head in range(kv * group, (kv + 1) * group):
                line = slice(head, head + 1)
                scores = nt_dot(keys, q_ref[:, head_columns(head)] * HEAD ** (-0.5))
                if own:
                    scores = jnp.where(causal(rows), scores, neg_large)
                    new_top = jnp.max(scores, axis=0, keepdims=True)
                else:
                    new_top = jnp.maximum(top[line, :], jnp.max(scores, axis=0, keepdims=True))
                weights_now = jnp.exp(scores - new_top)
                sums = jnp.sum(weights_now, axis=0, keepdims=True)
                mixed = tn_dot(values, weights_now.astype(jnp.bfloat16))
                if not own:
                    factor = jnp.exp(top[line, :] - new_top)
                    sums = sums + total[line, :] * factor
                    mixed = mixed + acc[head_columns(head), :] * factor
                top[line, :] = new_top
                total[line, :] = sums
                acc[head_columns(head), :] = mixed

    over_blocks(index_ref[0], update)
    log_ref[...] = jnp.zeros_like(log_ref)
    for head in range(HEADS):
        line = slice(head, head + 1)
        log_ref[line, :] = top[line, :] + jnp.log(total[line, :])
        acc[head_columns(head), :] = acc[head_columns(head), :] / total[line, :]
    attended = acc[...].T
    attended_ref[...] = attended
    mixed_ref[...] = attended.astype(jnp.bfloat16)


def attend_backward_kernel(
    index_ref, q_ref, blocks_ref, grads_ref, attended_ref, log_ref, query_ref, parts_ref, acc, delta
):
    rows = q_ref.shape[0]
    group = HEADS // KV_HEADS
    width = KV_HEADS * HEAD
    parts_ref[...] = jnp.zeros_like(parts_ref)
    acc[...] = (grads_ref[...].astype(jnp.float32) * attended_ref[...]).T
    for head in range(HEADS):
        delta[head : head + 1, :] = jnp.sum(acc[head_columns(head), :], axis=0, keepdims=True)
    acc[...] = jnp.zeros_like(acc)

    def update(j, own):
        for kv in range(KV_HEADS):
            keys = blocks_ref[j, :, head_columns(kv)]
            values = blocks_ref[j, :, head_columns(kv, width)]
            key_sum = jnp.zeros((rows, HEAD), jnp.float32)
            value_sum = jnp.zeros((rows, HEAD), jnp.float32)
            for head in range(kv * group, (kv + 1) * group):
                line = slice(head, head + 1)
                query = q_ref[:, head_columns(head)]
                grads = grads_ref[:, head_columns(head)]
                scores = nt_dot(keys, query * HEAD ** (-0.5))
                if own:
                    scores = jnp.where(causal(rows), scores, neg_large)
                probabilities = jnp.exp(scores - log_ref[line, :])
                grad_probs = nt_dot(values, grads)
                grad_scores = (
                    probabilities * (grad_probs - delta[line, :]) * HEAD ** (-0.5)
                ).astype(jnp.bfloat16)
                acc[head_columns(head), :] += tn_dot(keys, grad_scores)
                key_sum += jnp.dot(grad_scores, query, preferred_element_type=jnp.float32)
                value_sum += jnp.dot(
                    probabilities.astype(jnp.bfloat16), grads, preferred_element_type=jnp.float32
                )
            parts_ref[j, :, head_columns(kv)] = key_sum.astype(jnp.bfloat16)
            parts_ref[j, :, head_columns(kv, width)] = value_sum.astype(jnp.bfloat16)

    over_blocks(index_ref[0], update)
    query_ref[...] = acc[...].T


def in_vmem(count):
    return [pl.BlockSpec(memory_space=pltpu.VMEM)] * count


def attend_forward(query_rot, blocks, index):
    rows, width = query_rot.shape
    return pl.pallas_call(
        attend_forward_kernel,
        out_shape=(
            jax.ShapeDtypeStruct((rows, width), jnp.bfloat16),
            jax.ShapeDtypeStruct((rows, width), jnp.float32),
            jax.ShapeDtypeStruct((16, rows), jnp.float32),
        ),
        in_specs=[pl.BlockSpec(memory_space=pltpu.SMEM)] + in_vmem(2),
        out_specs=tuple(in_vmem(3)),
        scratch_shapes=[
            pltpu.VMEM((16, rows), jnp.float32),
            pltpu.VMEM((16, rows), jnp.float32),
            pltpu.VMEM((width, rows), jnp.float32),
        ],
        compiler_params=pltpu.CompilerParams(vmem_limit_bytes=WIDE),
        cost_estimate=pl.CostEstimate(
            flops=16 * rows * rows * width, bytes_accessed=2**22, transcendentals=36 * rows * rows
        ),
    )(index[None], query_rot, blocks)


def attend_backward(query_rot, blocks, grad_heads, attended, log_total, index):
    rows, width = query_rot.shape
    return pl.pallas_call(
        attend_backward_kernel,
        out_shape=(
            jax.ShapeDtypeStruct((rows, width), jnp.float32),
            jax.ShapeDtypeStruct(blocks.shape, jnp.bfloat16),
        ),
        in_specs=[pl.BlockSpec(memory_space=pltpu.SMEM)] + in_vmem(5),
        out_specs=tuple(in_vmem(2)),
        scratch_shapes=[
            pltpu.VMEM((width, rows), jnp.float32),
            pltpu.VMEM((16, rows), jnp.float32),
        ],
        compiler_params=pltpu.CompilerParams(vmem_limit_bytes=WIDE),
        cost_estimate=pl.CostEstimate(
            flops=40 * rows * rows * width, bytes_accessed=2**23, transcendentals=36 * rows * rows
        ),
    )(index[None], query_rot, blocks, grad_heads, attended, log_total)


def forward_attention(block_in, weights, tables, index):
    gain_attn, w_in, w_out, gain_ffn = weights
    tok_count, model_width = block_in.shape
    source = block_in.astype(jnp.float32)
    normed = (source * rms_scale(source) * gain_attn).astype(jnp.bfloat16)
    projected = linear(normed, w_in)
    query_width, key_width = HEADS * HEAD, KV_HEADS * HEAD
    query_rot = (
        rotate(projected[:, :query_width].reshape(1, tok_count, HEADS, HEAD), tables)
        .astype(jnp.bfloat16)
        .reshape(tok_count, query_width)
    )
    key_rot = (
        rotate(
            projected[:, query_width : query_width + key_width].reshape(
                1, tok_count, KV_HEADS, HEAD
            ),
            tables,
        )
        .astype(jnp.bfloat16)
        .reshape(tok_count, key_width)
    )
    values = projected[:, query_width + key_width :].astype(jnp.bfloat16)
    blocks = jnp.stack(gather_xor(jnp.concatenate([key_rot, values], axis=1)))
    return (source, normed, query_rot, blocks)


def forward_rest(source, normed, query_rot, blocks, weights, index):
    gain_attn, w_in, w_out, gain_ffn, w_gate_up, w_down = weights
    mixed_heads, attended, log_total = attend_forward(query_rot, blocks, index)
    hidden = source + linear(mixed_heads, w_out)
    normed_ffn = (hidden * rms_scale(hidden) * gain_ffn).astype(jnp.bfloat16)
    gate_up = linear(normed_ffn, w_gate_up)
    hidden_units = gate_up.shape[1] // 2
    gate_pre, upper = gate_up[:, :hidden_units], gate_up[:, hidden_units:]
    active = (gate_pre * jax.nn.sigmoid(gate_pre) * upper).astype(jnp.bfloat16)
    result = hidden + linear(active, w_down)
    kept = (
        source, normed, query_rot, blocks, log_total, mixed_heads, attended,
        hidden, normed_ffn, gate_up, active,
    )
    return (result, kept)


def backward_ffn(kept, grad_out, weights):
    gain_attn, w_in, w_out, gain_ffn, w_gate_up, w_down = weights
    hidden, normed_ffn, gate_up, active = kept[7:]
    hidden_units = gate_up.shape[1] // 2
    gate_pre, upper = gate_up[:, :hidden_units], gate_up[:, hidden_units:]
    grad_ffn_out = grad_out.astype(jnp.bfloat16)
    grad_active = input_grad(grad_ffn_out, w_down)
    sigmoid_gate = jax.nn.sigmoid(gate_pre)
    grad_gate = (
        grad_active * upper * sigmoid_gate * (1.0 + gate_pre * (1.0 - sigmoid_gate))
    ).astype(jnp.bfloat16)
    grad_upper = (grad_active * gate_pre * sigmoid_gate).astype(jnp.bfloat16)
    grad_both = jnp.concatenate([grad_gate, grad_upper], axis=1)
    g_down = weight_grad(active, grad_ffn_out).astype(jnp.bfloat16)
    g_gate_up = weight_grad(normed_ffn, grad_both).astype(jnp.bfloat16)
    grad_normed_ffn = input_grad(grad_both, w_gate_up)
    grad_part, g_gain_ffn = rms_back(hidden, gain_ffn, grad_normed_ffn)
    return (grad_out + grad_part, g_gain_ffn, g_gate_up, g_down)


def backward_attention(kept, grad_hidden, weights, tables, index, pending=()):
    gain_attn, w_in, w_out, gain_ffn, w_gate_up, w_down = weights
    source, normed, query_rot, blocks, log_total, mixed_heads, attended = kept[:7]
    tok_count = source.shape[0]
    grad_attn = grad_hidden.astype(jnp.bfloat16)
    g_out = weight_grad(mixed_heads, grad_attn)
    grad_heads = input_grad(grad_attn, w_out).astype(jnp.bfloat16)
    grad_query, parts = attend_backward(
        query_rot, blocks, grad_heads, attended, log_total, index
    )
    parts, pending = tied(parts, pending)
    received = xor_send(parts[1::2], "shard", 1)
    own_sum = add_low(parts[0], received[0])
    cross_sum = add_low(parts[2], received[1])
    key_width = KV_HEADS * HEAD
    grad_kv = own_sum.astype(jnp.float32) + xor_send(cross_sum, "shard", 2).astype(jnp.float32)
    grad_query_rows = (
        rotate_back(grad_query.reshape(1, tok_count, HEADS, HEAD), tables)
        .astype(jnp.bfloat16)
        .reshape(tok_count, HEADS * HEAD)
    )
    grad_key_rows = (
        rotate_back(grad_kv[:, :key_width].reshape(1, tok_count, KV_HEADS, HEAD), tables)
        .astype(jnp.bfloat16)
        .reshape(tok_count, key_width)
    )
    grad_rows = jnp.concatenate(
        [grad_query_rows, grad_key_rows, grad_kv[:, key_width:].astype(jnp.bfloat16)], axis=1
    )
    g_in = weight_grad(normed, grad_rows)
    grad_normed = input_grad(grad_rows, w_in)
    grad_part, g_gain_attn = rms_back(source, gain_attn, grad_normed)
    return (grad_hidden + grad_part, g_gain_attn, g_in, g_out, pending)


def both_sections(
    ends, attn_norm, w_query, w_key, w_value, w_out, ffn_norm, w_gate, w_up, w_down
):
    section = lax.axis_index("section")
    leading = section == 0
    index = lax.axis_index("shard")
    replica = lax.axis_index("replica")
    local = ends[0]
    tok_count, model_width = local.shape[-2:]
    own_pair = local.reshape(2, tok_count, model_width)
    moved = xor_send(
        lax.dynamic_index_in_dim(own_pair, 1 - section, 0, keepdims=False), "section", 1
    )
    stayed = lax.dynamic_index_in_dim(own_pair, section, 0, keepdims=False)
    tokens = jnp.where(leading, stayed, moved)
    cotangent = jnp.where(leading, moved, stayed)

    attn_width = w_query.shape[2] + 2 * w_key.shape[2] + w_out.shape[2]
    in_width = attn_width - w_out.shape[2]
    gains = jnp.stack([attn_norm[0], ffn_norm[0]], axis=1)
    groups = (
        jnp.concatenate([w_query[0], w_key[0], w_value[0], w_out[0], gains], axis=1),
        jnp.concatenate([w_gate[0], w_up[0]], axis=1),
        w_down[0],
    )
    positions = index * tok_count + jnp.arange(tok_count, dtype=jnp.int32)
    tables = rotation_tables(positions)
    other_attn = xor_send(groups[0], "section", 1)
    own_rest, other_attn = tied(groups[1:], other_attn)
    other_rest = tuple(xor_send(group, "section", 1) for group in own_rest)

    def of_layer(layer, own, other):
        return jnp.where(section == layer, own, other)

    def attn_weights(layer, own, other):
        attn = gather_rows(of_layer(layer, own, other), index)
        return (
            attn[:, attn_width].astype(jnp.float32),
            attn[:, :in_width],
            attn[:, in_width:attn_width],
            attn[:, attn_width + 1].astype(jnp.float32),
        )

    attn_first = attn_weights(0, groups[0], other_attn)
    first_state = forward_attention(tokens, attn_first, tables, index)
    first_rest, sent_blocks = tied(
        tuple(of_layer(0, own, other) for own, other in zip(own_rest, other_rest)), first_state[3]
    )
    first_state = first_state[:3] + (sent_blocks,)
    first_rest = tuple(gather_rows(group, index) for group in first_rest)
    second_own, second_other, first_rest = tied(groups, (other_attn,) + other_rest, first_rest)
    weights_first = attn_first + first_rest
    attn_second = attn_weights(1, second_own[0], second_other[0])
    middle, kept_first = forward_rest(*first_state, weights_first, index)
    second_state = forward_attention(middle.astype(jnp.bfloat16), attn_second, tables, index)
    second_rest = tuple(
        gather_rows(of_layer(1, own, other), index)
        for own, other in zip(second_own[1:], second_other[1:])
    )
    weights_second = attn_second + second_rest
    final, kept_second = forward_rest(*second_state, weights_second, index)
    final_arrived = lax.ppermute(final.astype(jnp.bfloat16), "section", [(0, 1)])

    def pack(g_in, g_out, g_gain_attn, g_gain_ffn):
        pad = jnp.zeros((model_width, 2048 - attn_width - 2), jnp.float32)
        return jnp.concatenate(
            [g_in, g_out, g_gain_attn[:, None], g_gain_ffn[:, None], pad], axis=1
        ).astype(jnp.bfloat16)

    def over_shards(*partials):
        return tuple(reduce_to_owner(partial, index) for partial in partials)

    def over_replicas(gate_up, down):
        return (reduce_replicas(gate_up, replica, 1), reduce_replicas(down, replica, 0))

    grad_hidden, g_gain_ffn, g_gate_up, g_down = backward_ffn(
        kept_second, cotangent.astype(jnp.float32), weights_second
    )
    ffn_second = over_shards(g_gate_up, g_down)
    grad, g_gain_attn, g_in, g_out, _ = backward_attention(
        kept_second, grad_hidden, weights_second, tables, index
    )
    grad, ffn_second = tied(grad.astype(jnp.bfloat16), ffn_second)
    ffn_second = over_replicas(*ffn_second)
    (attn_second_sum,) = over_shards(pack(g_in, g_out, g_gain_attn, g_gain_ffn))
    grad_hidden, g_gain_ffn, g_gate_up, g_down = backward_ffn(
        kept_first, grad.astype(jnp.float32), weights_first
    )
    grad_hidden, ffn_second, attn_second_sum = tied(grad_hidden, ffn_second, attn_second_sum)
    ffn_second = tuple(reduce_sections(value, 1) for value in ffn_second)
    attn_second_sum = reduce_sections(reduce_replicas(attn_second_sum, replica, 1), 1)
    ffn_first = over_shards(g_gate_up, g_down)
    grad, g_gain_attn, g_in, g_out, (ffn_first, ffn_second, attn_second_sum) = backward_attention(
        kept_first, grad_hidden, weights_first, tables, index,
        (ffn_first, ffn_second, attn_second_sum),
    )
    ffn_first = tuple(reduce_sections(value, 0) for value in over_replicas(*ffn_first))
    (attn_first_sum,) = over_shards(pack(g_in, g_out, g_gain_attn, g_gain_ffn))
    attn_first_sum = reduce_sections(reduce_replicas(attn_first_sum, replica, 1), 0)
    quarters = ((attn_second_sum,) + ffn_second, (attn_first_sum,) + ffn_first)
    grad_arrived = lax.ppermute(grad.astype(jnp.bfloat16), "section", [(1, 0)])
    attn_sum, gate_up_sum, down_sum = [
        gather_replicas(jnp.where(leading, first, second), replica, axis).astype(jnp.float32)
        for first, second, axis in zip(quarters[1], quarters[0], (1, 1, 0))
    ]
    ends_out = jnp.stack(
        [
            jnp.where(leading, grad, final_arrived.astype(jnp.float32)),
            jnp.where(leading, grad_arrived.astype(jnp.float32), final),
        ]
    ).reshape(1, 2, 1, tok_count, model_width)
    cuts = [w_query.shape[2], w_query.shape[2] + w_key.shape[2], in_width, attn_width]
    g_query, g_key, g_value, g_out, _ = jnp.split(attn_sum, cuts, axis=1)
    units = w_gate.shape[2]
    return (
        ends_out,
        attn_sum[:, attn_width][None],
        g_query[None],
        g_key[None],
        g_value[None],
        g_out[None],
        attn_sum[:, attn_width + 1][None],
        gate_up_sum[:, :units][None],
        gate_up_sum[:, units:][None],
        down_sum[None],
    )


def solution(mesh):
    balanced = (
        mesh.shape["section"] == 2 and mesh.shape["replica"] == 4 and mesh.shape["shard"] == 4
    )
    program = both_sections if balanced else on_device
    return jax.shard_map(
        program,
        mesh=mesh,
        in_specs=(
            P("section", None, "replica", "shard", None),
            P("section", "shard"),
            P("section", "shard", None),
            P("section", "shard", None),
            P("section", "shard", None),
            P("section", "shard", None),
            P("section", "shard"),
            P("section", "shard", None),
            P("section", "shard", None),
            P("section", "shard", None),
        ),
        out_specs=(
            P("section", None, "replica", "shard", None),
            P("section", "shard"),
            P("section", "shard", None),
            P("section", "shard", None),
            P("section", "shard", None),
            P("section", "shard", None),
            P("section", "shard"),
            P("section", "shard", None),
            P("section", "shard", None),
            P("section", "shard", None),
        ),
        check_vma=False,
    )
```

```python
from functools import partial

import jax
import jax.numpy as jnp
from jax import lax
from jax.experimental import pallas as pl
from jax.experimental.pallas import tpu as pltpu
from jax.sharding import PartitionSpec as P

HEADS = 9
KV_HEADS = 3
HEAD = 64


epsilon = 1e-05
rope_base = 100000.0
neg_large = -1e30


def shifted(shard, axis, by):
    peers = lax.axis_size(axis)
    pairs = [(i, i + by) for i in range(peers) if 0 <= i + by < peers]
    return lax.ppermute(shard, axis, pairs)


def rms_scale(source):
    return lax.rsqrt(jnp.mean(source * source, axis=-1, keepdims=True) + epsilon)


def rms_back(source, gain_vector, grad_normed):
    inv_scale = rms_scale(source)
    unit_rows = source * inv_scale
    grad_unit = grad_normed * gain_vector
    gain_grad = jnp.sum(grad_normed * unit_rows, axis=0)
    grad_source = inv_scale * (
        grad_unit - unit_rows * jnp.mean(grad_unit * unit_rows, axis=-1, keepdims=True)
    )
    return (grad_source, gain_grad)


def rotation_tables(positions):
    half_size = HEAD // 2
    frequency = rope_base ** (-jnp.arange(half_size, dtype=jnp.float32) * 2.0 / HEAD)
    angles = positions.astype(jnp.float32)[:, None] * frequency[None, :]
    return (jnp.cos(angles)[None, :, None, :], jnp.sin(angles)[None, :, None, :])


def rotate(tensor, tables):
    cosine, sine_part = tables
    half_size = tensor.shape[-1] // 2
    first_half = tensor[..., :half_size]
    second_half = tensor[..., half_size:]
    return jnp.concatenate(
        [
            first_half * cosine - second_half * sine_part,
            second_half * cosine + first_half * sine_part,
        ],
        axis=-1,
    )


def rotate_back(gradient, tables):
    cosine, sine_part = tables
    half_size = gradient.shape[-1] // 2
    first_half = gradient[..., :half_size]
    second_half = gradient[..., half_size:]
    return jnp.concatenate(
        [
            first_half * cosine + second_half * sine_part,
            second_half * cosine - first_half * sine_part,
        ],
        axis=-1,
    )


def linear(left_side, right_side):
    return jnp.dot(left_side, right_side, preferred_element_type=jnp.float32)


def weight_grad(left_side, right_side):
    return jnp.einsum("rd,rf->df", left_side, right_side, preferred_element_type=jnp.float32)


def input_grad(gradient, weight):
    return jnp.einsum("rf,df->rd", gradient, weight, preferred_element_type=jnp.float32)


def split_blocks(tensor):
    seq_count, length, head_count, head_size = tensor.shape
    block_rows = min(512, length)
    shaped = tensor.reshape(seq_count, length // block_rows, block_rows, head_count, head_size)
    return (jnp.moveaxis(shaped, 1, 0), block_rows)


def block_scores(grouped, key_block, block_start, positions):
    raw_scores = jnp.einsum(
        "stkgd,sukd->skgtu", grouped, key_block, preferred_element_type=jnp.float32
    )
    key_pos = block_start + jnp.arange(key_block.shape[1], dtype=jnp.int32)
    allowed = key_pos[None, :] <= positions[:, None]
    return (jnp.where(allowed, raw_scores * HEAD ** (-0.5), neg_large), allowed)


def keep_carry(state_triple):
    return state_triple


def scatter_at_end(parts):
    attn_shares = (
        lax.psum_scatter(
            parts[0].astype(jnp.bfloat16), "shard", scatter_dimension=0, tiled=True
        ).astype(jnp.float32),
        lax.psum_scatter(
            parts[1].astype(jnp.bfloat16), "shard", scatter_dimension=0, tiled=True
        ).astype(jnp.float32),
        lax.psum_scatter(
            parts[2].astype(jnp.bfloat16), "shard", scatter_dimension=0, tiled=True
        ).astype(jnp.float32),
        lax.psum_scatter(
            parts[3].astype(jnp.bfloat16), "shard", scatter_dimension=0, tiled=True
        ).astype(jnp.float32),
        lax.psum_scatter(
            parts[4].astype(jnp.bfloat16), "shard", scatter_dimension=0, tiled=True
        ).astype(jnp.float32),
        lax.psum_scatter(
            parts[5].astype(jnp.bfloat16), "shard", scatter_dimension=0, tiled=True
        ).astype(jnp.float32),
    )
    ffn_shares = (
        lax.psum_scatter(
            parts[6].astype(jnp.bfloat16), "shard", scatter_dimension=0, tiled=True
        ).astype(jnp.float32),
        lax.psum_scatter(
            parts[7].astype(jnp.bfloat16), "shard", scatter_dimension=0, tiled=True
        ).astype(jnp.float32),
    )
    down_share = lax.psum_scatter(
        parts[8].astype(jnp.bfloat16), "shard", scatter_dimension=0, tiled=True
    ).astype(jnp.float32)
    return tuple(attn_shares) + tuple(ffn_shares) + (down_share,)


def forward_layer(block_in, weights, tables, positions):
    gain_attn, w_query, w_key, w_value, w_out, gain_ffn, w_gate, w_up, w_down = weights
    seq_count, tok_count, model_width = block_in.shape
    group_size = HEADS // KV_HEADS
    source = block_in.astype(jnp.float32).reshape(seq_count * tok_count, model_width)
    normed = (source * rms_scale(source) * gain_attn.astype(jnp.float32)).astype(jnp.bfloat16)
    query_rot = rotate(
        linear(normed, w_query).reshape(seq_count, tok_count, HEADS, HEAD), tables
    ).astype(jnp.bfloat16)
    key_rot = rotate(
        linear(normed, w_key).reshape(seq_count, tok_count, KV_HEADS, HEAD), tables
    ).astype(jnp.bfloat16)
    values = (
        linear(normed, w_value).astype(jnp.bfloat16).reshape(seq_count, tok_count, KV_HEADS, HEAD)
    )
    keys_all, values_all = (
        lax.all_gather(key_rot, "shard", axis=1, tiled=True),
        lax.all_gather(values, "shard", axis=1, tiled=True),
    )
    grouped = query_rot.reshape(seq_count, tok_count, KV_HEADS, group_size, HEAD)
    key_blocks, block_rows = split_blocks(keys_all)
    value_blocks, block_rows = split_blocks(values_all)
    block_ids = jnp.arange(key_blocks.shape[0], dtype=jnp.int32)
    last_query = positions[-1]

    def attend_step(state_triple, block_args):
        key_block, value_block, block_index = block_args
        block_start = block_index * block_rows

        def attend_update(state_triple):
            running_top, running_sum, mixed_sum = state_triple
            scores, allowed = block_scores(grouped, key_block, block_start, positions)
            new_top = jnp.maximum(running_top, jnp.max(scores, axis=-1))
            weights_now = jnp.where(allowed, jnp.exp(scores - new_top[..., None]), 0.0)
            factor = jnp.exp(running_top - new_top)
            running_sum = running_sum * factor + jnp.sum(weights_now, axis=-1)
            mixed_sum = mixed_sum * jnp.moveaxis(factor, 3, 1)[..., None] + jnp.einsum(
                "skgtu,sukd->stkgd",
                weights_now.astype(jnp.bfloat16),
                value_block,
                preferred_element_type=jnp.float32,
            )
            return (new_top, running_sum, mixed_sum)

        return (lax.cond(block_start <= last_query, attend_update, keep_carry, state_triple), None)

    stats_shape = (seq_count, KV_HEADS, group_size, tok_count)
    start_triple = (
        jnp.full(stats_shape, neg_large, jnp.float32),
        jnp.zeros(stats_shape, jnp.float32),
        jnp.zeros(grouped.shape, jnp.float32),
    )
    (running_top, running_sum, mixed_sum), unused = lax.scan(
        attend_step, start_triple, (key_blocks, value_blocks, block_ids)
    )
    log_total = running_top + jnp.log(running_sum)
    attended = mixed_sum / jnp.moveaxis(running_sum, 3, 1)[..., None]
    mixed_heads = attended.astype(jnp.bfloat16).reshape(seq_count * tok_count, HEADS * HEAD)
    hidden = source + linear(mixed_heads, w_out)
    normed_ffn = (hidden * rms_scale(hidden) * gain_ffn.astype(jnp.float32)).astype(jnp.bfloat16)
    gate_pre = linear(normed_ffn, w_gate)
    upper = linear(normed_ffn, w_up)
    active = (gate_pre * jax.nn.sigmoid(gate_pre) * upper).astype(jnp.bfloat16)
    result = hidden + linear(active, w_down)
    kept_state = (
        block_in,
        normed,
        grouped,
        key_blocks,
        value_blocks,
        log_total,
        mixed_heads,
        attended,
        hidden,
        normed_ffn,
        gate_pre,
        upper,
        active,
    )
    return (result, kept_state)


def backward_layer(kept_state, grad_out, weights, tables, positions):
    gain_attn, w_query, w_key, w_value, w_out, gain_ffn, w_gate, w_up, w_down = weights
    (
        block_in,
        normed,
        grouped,
        key_blocks,
        value_blocks,
        log_total,
        mixed_heads,
        attended,
        hidden,
        normed_ffn,
        gate_pre,
        upper,
        active,
    ) = kept_state
    seq_count, tok_count, model_width = block_in.shape
    block_rows = key_blocks.shape[2]
    source = block_in.astype(jnp.float32).reshape(seq_count * tok_count, model_width)
    grad_ffn_out = grad_out.astype(jnp.bfloat16)
    g_down = weight_grad(active, grad_ffn_out)
    grad_active = input_grad(grad_ffn_out, w_down)
    sigmoid_gate = jax.nn.sigmoid(gate_pre)
    grad_gate = (
        grad_active * upper * sigmoid_gate * (1.0 + gate_pre * (1.0 - sigmoid_gate))
    ).astype(jnp.bfloat16)
    grad_upper = (grad_active * gate_pre * sigmoid_gate).astype(jnp.bfloat16)
    g_gate = weight_grad(normed_ffn, grad_gate)
    g_up = weight_grad(normed_ffn, grad_upper)
    grad_normed_ffn = input_grad(grad_gate, w_gate) + input_grad(grad_upper, w_up)
    grad_hidden_part, g_gain_ffn = rms_back(hidden, gain_ffn.astype(jnp.float32), grad_normed_ffn)
    grad_hidden = grad_out + grad_hidden_part
    grad_attn = grad_hidden.astype(jnp.bfloat16)
    g_out = weight_grad(mixed_heads, grad_attn)
    grad_heads = input_grad(grad_attn, w_out).astype(jnp.bfloat16).reshape(grouped.shape)
    row_delta = jnp.moveaxis(jnp.sum(grad_heads.astype(jnp.float32) * attended, axis=-1), 1, 3)
    block_ids = jnp.arange(key_blocks.shape[0], dtype=jnp.int32)
    last_query = positions[-1]

    def grad_step(grad_query, block_args):
        key_block, value_block, block_index = block_args
        block_start = block_index * block_rows

        def grad_update(grad_query):
            scores, allowed = block_scores(grouped, key_block, block_start, positions)
            probabilities = jnp.where(allowed, jnp.exp(scores - log_total[..., None]), 0.0)
            grad_probs = jnp.einsum(
                "stkgd,sukd->skgtu", grad_heads, value_block, preferred_element_type=jnp.float32
            )
            grad_scores = (
                probabilities * (grad_probs - row_delta[..., None]) * HEAD ** (-0.5)
            ).astype(jnp.bfloat16)
            grad_query = grad_query + jnp.einsum(
                "skgtu,sukd->stkgd", grad_scores, key_block, preferred_element_type=jnp.float32
            )
            grad_key_block = jnp.einsum(
                "skgtu,stkgd->sukd", grad_scores, grouped, preferred_element_type=jnp.float32
            )
            grad_value_block = jnp.einsum(
                "skgtu,stkgd->sukd",
                probabilities.astype(jnp.bfloat16),
                grad_heads,
                preferred_element_type=jnp.float32,
            )
            return (grad_query, (grad_key_block, grad_value_block))

        def skip_block(grad_query):
            empty_grad = jnp.zeros(key_block.shape, jnp.float32)
            return (grad_query, (empty_grad, empty_grad))

        return lax.cond(block_start <= last_query, grad_update, skip_block, grad_query)

    grad_query, (key_parts, value_parts) = lax.scan(
        grad_step, jnp.zeros(grouped.shape, jnp.float32), (key_blocks, value_blocks, block_ids)
    )
    full_shape = (seq_count, key_parts.shape[0] * block_rows, KV_HEADS, HEAD)
    key_full = jnp.moveaxis(key_parts, 0, 1).reshape(full_shape)
    value_full = jnp.moveaxis(value_parts, 0, 1).reshape(full_shape)
    grad_keys, grad_values = (
        lax.psum_scatter(
            key_full.astype(jnp.bfloat16), "shard", scatter_dimension=1, tiled=True
        ).astype(jnp.float32),
        lax.psum_scatter(
            value_full.astype(jnp.bfloat16), "shard", scatter_dimension=1, tiled=True
        ).astype(jnp.float32),
    )
    row_count = seq_count * tok_count
    grad_query_rows = (
        rotate_back(grad_query.reshape(seq_count, tok_count, HEADS, HEAD), tables)
        .astype(jnp.bfloat16)
        .reshape(row_count, HEADS * HEAD)
    )
    grad_key_rows = (
        rotate_back(grad_keys, tables).astype(jnp.bfloat16).reshape(row_count, KV_HEADS * HEAD)
    )
    grad_value_rows = grad_values.astype(jnp.bfloat16).reshape(row_count, KV_HEADS * HEAD)
    g_query = weight_grad(normed, grad_query_rows)
    g_key = weight_grad(normed, grad_key_rows)
    g_value = weight_grad(normed, grad_value_rows)
    grad_normed = (
        input_grad(grad_query_rows, w_query)
        + input_grad(grad_key_rows, w_key)
        + input_grad(grad_value_rows, w_value)
    )
    grad_source_part, g_gain_attn = rms_back(source, gain_attn.astype(jnp.float32), grad_normed)
    grad_source = grad_hidden + grad_source_part
    return (
        grad_source,
        (g_gain_attn, g_query, g_key, g_value, g_out, g_gain_ffn, g_gate, g_up, g_down),
    )


def on_device(ends, attn_norm, w_query, w_key, w_value, w_out, ffn_norm, w_gate, w_up, w_down):
    params = (
        attn_norm[0],
        w_query[0],
        w_key[0],
        w_value[0],
        w_out[0],
        ffn_norm[0],
        w_gate[0],
        w_up[0],
        w_down[0],
    )
    leading = lax.axis_index("section") == 0
    held_weights = (
        lax.all_gather(params[0], "shard", axis=0, tiled=True),
        lax.all_gather(params[1], "shard", axis=0, tiled=True),
        lax.all_gather(params[2], "shard", axis=0, tiled=True),
        lax.all_gather(params[3], "shard", axis=0, tiled=True),
        lax.all_gather(params[4], "shard", axis=0, tiled=True),
        lax.all_gather(params[5], "shard", axis=0, tiled=True),
        lax.all_gather(params[6], "shard", axis=0, tiled=True),
        lax.all_gather(params[7], "shard", axis=0, tiled=True),
        lax.all_gather(params[8], "shard", axis=0, tiled=True),
    )
    local_ends = ends[0]
    micro_count, seq_count, tok_count, model_width = local_ends.shape
    positions = lax.axis_index("shard") * tok_count + jnp.arange(tok_count, dtype=jnp.int32)
    tables = rotation_tables(positions)
    arriving = jnp.zeros((seq_count, tok_count, model_width), jnp.bfloat16)
    kept_states = []
    layer_outputs = []
    for moment in range(micro_count + 1):
        own_rows = local_ends[moment] if moment < micro_count else jnp.zeros_like(arriving)
        block_in = jnp.where(leading, own_rows, arriving)
        result, kept_state = forward_layer(block_in, held_weights, tables, positions)
        kept_states.append(kept_state)
        if moment > 0:
            layer_outputs.append(result)
        if moment < micro_count:
            arriving = shifted(
                result.astype(jnp.bfloat16).reshape(seq_count, tok_count, model_width), "section", 1
            )
    returning = jnp.zeros((seq_count * tok_count, model_width), jnp.float32)
    totals = None
    input_grads = []
    for moment in range(micro_count + 1):
        earlier = moment - 1 if moment > 0 else micro_count
        later = moment + 1 if moment < micro_count else 0
        kept_state = jax.tree.map(
            partial(jnp.where, leading), kept_states[earlier], kept_states[later]
        )
        if moment < micro_count:
            own_grad = (
                local_ends[moment].astype(jnp.float32).reshape(seq_count * tok_count, model_width)
            )
        else:
            own_grad = jnp.zeros_like(returning)
        grad_source, grad_parts = backward_layer(
            kept_state, jnp.where(leading, returning, own_grad), held_weights, tables, positions
        )
        totals = grad_parts if totals is None else jax.tree.map(jnp.add, totals, grad_parts)
        if moment > 0:
            input_grads.append(grad_source)
        if moment < micro_count:
            returning = shifted(grad_source.astype(jnp.bfloat16), "section", -1).astype(jnp.float32)
    pieces = [
        jnp.where(leading, input_grads[number], layer_outputs[number])
        for number in range(micro_count)
    ]
    ends_out = jnp.stack(pieces).reshape(1, micro_count, seq_count, tok_count, model_width)
    shares = scatter_at_end(totals)
    summed = (
        lax.psum(shares[0].astype(jnp.bfloat16), "replica").astype(jnp.float32),
        lax.psum(shares[1].astype(jnp.bfloat16), "replica").astype(jnp.float32),
        lax.psum(shares[2].astype(jnp.bfloat16), "replica").astype(jnp.float32),
        lax.psum(shares[3].astype(jnp.bfloat16), "replica").astype(jnp.float32),
        lax.psum(shares[4].astype(jnp.bfloat16), "replica").astype(jnp.float32),
        lax.psum(shares[5].astype(jnp.bfloat16), "replica").astype(jnp.float32),
        lax.psum(shares[6].astype(jnp.bfloat16), "replica").astype(jnp.float32),
        lax.psum(shares[7].astype(jnp.bfloat16), "replica").astype(jnp.float32),
        lax.psum(shares[8].astype(jnp.bfloat16), "replica").astype(jnp.float32),
    )
    return (ends_out,) + tuple((share[None] for share in summed))


def xor_send(value, axis, bits):
    peers = lax.axis_size(axis)
    return lax.ppermute(value, axis, [(i, i ^ bits) for i in range(peers)])


def xor_sort(parts, index):
    low_bit, high_bit = (index & 1) == 1, (index & 2) == 2
    a, b, c, d = parts
    pairs = (
        jnp.where(low_bit, b, a),
        jnp.where(low_bit, a, b),
        jnp.where(low_bit, d, c),
        jnp.where(low_bit, c, d),
    )
    return (
        jnp.where(high_bit, pairs[2], pairs[0]),
        jnp.where(high_bit, pairs[3], pairs[1]),
        jnp.where(high_bit, pairs[0], pairs[2]),
        jnp.where(high_bit, pairs[1], pairs[3]),
    )


def gather_xor(value):
    crossed = xor_send(value, "shard", 2)
    beside = xor_send(value, "shard", 1)
    far = xor_send(crossed, "shard", 1)
    return (value, beside, crossed, far)


def gather_rows(value, index):
    return jnp.concatenate(xor_sort(gather_xor(value), index), axis=0)


def add_low(first, second):
    return (first.astype(jnp.float32) + second.astype(jnp.float32)).astype(jnp.bfloat16)


def reduce_to_owner(partial, index):
    rows = partial.shape[0] // 4
    core, chip = index & 1, index >> 1

    def block(number):
        return lax.dynamic_slice_in_dim(partial, number * rows, rows, 0)

    far, near = [
        add_low(block(2 * owner + core), xor_send(block(2 * owner + (core ^ 1)), "shard", 1))
        for owner in (chip ^ 1, chip)
    ]
    return add_low(near, xor_send(far, "shard", 2))


FOLD = ((0, 2, 3, 1), (1, 3, 2, 0))


def section_pairs(half, moves, back):
    pairs = []
    for start, end in moves:
        for held, folded in enumerate(FOLD[half]):
            ends = (start * 4 + held, end * 4 + folded)
            if back:
                ends = (start * 4 + folded, end * 4 + held)
            pairs.append(ends)
    return pairs


def fold_rows(rows, index, moves):
    size = rows.shape[0] // 2
    first, second = [
        lax.ppermute(
            rows[half * size : (half + 1) * size],
            ("section", "shard"),
            section_pairs(half, moves, False),
        )
        for half in (0, 1)
    ]
    odd = (index & 1) == 1
    return jnp.concatenate([jnp.where(odd, second, first), jnp.where(odd, first, second)], axis=0)


def unfold_rows(rows, index, moves):
    size = rows.shape[0] // 2
    low, high = rows[:size], rows[size:]
    odd = (index & 1) == 1
    parts = (jnp.where(odd, high, low), jnp.where(odd, low, high))
    return jnp.concatenate(
        [
            lax.ppermute(parts[half], ("section", "shard"), section_pairs(half, moves, True))
            for half in (0, 1)
        ],
        axis=0,
    )


def reduce_replicas(value, replica, axis):
    size = value.shape[axis] // 4

    def quarter(number):
        return lax.dynamic_slice_in_dim(value, number * size, size, axis)

    total = quarter(replica).astype(jnp.float32)
    for bits in (1, 2, 3):
        total = total + xor_send(quarter(replica ^ bits), "replica", bits).astype(jnp.float32)
    return total.astype(jnp.bfloat16)


def gather_replicas(value, replica, axis):
    parts = (value,) + tuple(xor_send(value, "replica", bits) for bits in (1, 2, 3))
    return jnp.concatenate(xor_sort(parts, replica), axis=axis)


def reduce_sections(value, layer):
    return add_low(value, lax.ppermute(value, "section", [(1 - layer, layer)]))


def tied(*values):
    return lax.optimization_barrier(values)


WIDE = 50 * 2**20


def nt_dot(left, right):
    return lax.dot_general(left, right, (((1,), (1,)), ((), ())), preferred_element_type=jnp.float32)


def tn_dot(left, right):
    return lax.dot_general(left, right, (((0,), (0,)), ((), ())), preferred_element_type=jnp.float32)


def head_columns(head, start=0):
    return slice(start + head * HEAD, start + (head + 1) * HEAD)


def over_blocks(index, rows, update):
    every, early, late = slice(0, rows), slice(0, rows // 2), slice(rows // 2, rows)
    update(0, True, every, every)

    def other(j, carry):
        before = (index ^ j) < index

        @pl.when(before)
        def _():
            update(j, False, early, every)

        @pl.when(jnp.logical_not(before))
        def _():
            update(j, False, every, late)

        return carry

    lax.fori_loop(1, 4, other, 0)


def causal(rows):
    keys = lax.broadcasted_iota(jnp.int32, (rows, rows), 0)
    queries = lax.broadcasted_iota(jnp.int32, (rows, rows), 1)
    return keys <= queries


def attend_forward_kernel(index_ref, q_ref, blocks_ref, mixed_ref, attended_ref, log_ref, top, total, acc):
    rows = q_ref.shape[0]
    group = HEADS // KV_HEADS

    def update(j, own, met, asked):
        for kv in range(KV_HEADS):
            keys = blocks_ref[j, met, head_columns(kv)]
            values = blocks_ref[j, met, head_columns(kv, KV_HEADS * HEAD)]
            for head in range(kv * group, (kv + 1) * group):
                line = slice(head, head + 1)
                scores = nt_dot(keys, q_ref[asked, head_columns(head)] * HEAD ** (-0.5))
                if own:
                    scores = jnp.where(causal(rows), scores, neg_large)
                    new_top = jnp.max(scores, axis=0, keepdims=True)
                else:
                    new_top = jnp.maximum(top[line, asked], jnp.max(scores, axis=0, keepdims=True))
                weights_now = jnp.exp(scores - new_top)
                sums = jnp.sum(weights_now, axis=0, keepdims=True)
                mixed = tn_dot(values, weights_now.astype(jnp.bfloat16))
                if not own:
                    factor = jnp.exp(top[line, asked] - new_top)
                    sums = sums + total[line, asked] * factor
                    mixed = mixed + acc[head_columns(head), asked] * factor
                top[line, asked] = new_top
                total[line, asked] = sums
                acc[head_columns(head), asked] = mixed

    over_blocks(index_ref[0], rows, update)
    log_ref[...] = jnp.zeros_like(log_ref)
    for head in range(HEADS):
        line = slice(head, head + 1)
        log_ref[line, :] = top[line, :] + jnp.log(total[line, :])
        acc[head_columns(head), :] = acc[head_columns(head), :] / total[line, :]
    attended = acc[...].T
    attended_ref[...] = attended
    mixed_ref[...] = attended.astype(jnp.bfloat16)


def attend_backward_kernel(
    index_ref, q_ref, blocks_ref, grads_ref, attended_ref, log_ref, query_ref, parts_ref, acc, delta
):
    rows = q_ref.shape[0]
    group = HEADS // KV_HEADS
    width = KV_HEADS * HEAD
    parts_ref[...] = jnp.zeros_like(parts_ref)
    acc[...] = (grads_ref[...].astype(jnp.float32) * attended_ref[...]).T
    for head in range(HEADS):
        delta[head : head + 1, :] = jnp.sum(acc[head_columns(head), :], axis=0, keepdims=True)
    acc[...] = jnp.zeros_like(acc)

    def update(j, own, met, asked):
        for kv in range(KV_HEADS):
            keys = blocks_ref[j, met, head_columns(kv)]
            values = blocks_ref[j, met, head_columns(kv, width)]
            key_sum = jnp.zeros((met.stop - met.start, HEAD), jnp.float32)
            value_sum = jnp.zeros((met.stop - met.start, HEAD), jnp.float32)
            for head in range(kv * group, (kv + 1) * group):
                line = slice(head, head + 1)
                query = q_ref[asked, head_columns(head)]
                grads = grads_ref[asked, head_columns(head)]
                scores = nt_dot(keys, query * HEAD ** (-0.5))
                if own:
                    scores = jnp.where(causal(rows), scores, neg_large)
                probabilities = jnp.exp(scores - log_ref[line, asked])
                grad_probs = nt_dot(values, grads)
                grad_scores = (
                    probabilities * (grad_probs - delta[line, asked]) * HEAD ** (-0.5)
                ).astype(jnp.bfloat16)
                acc[head_columns(head), asked] += tn_dot(keys, grad_scores)
                key_sum += jnp.dot(grad_scores, query, preferred_element_type=jnp.float32)
                value_sum += jnp.dot(
                    probabilities.astype(jnp.bfloat16), grads, preferred_element_type=jnp.float32
                )
            parts_ref[j, met, head_columns(kv)] = key_sum.astype(jnp.bfloat16)
            parts_ref[j, met, head_columns(kv, width)] = value_sum.astype(jnp.bfloat16)

    over_blocks(index_ref[0], rows, update)
    query_ref[...] = acc[...].T


def in_vmem(count):
    return [pl.BlockSpec(memory_space=pltpu.VMEM)] * count


def attend_forward(query_rot, blocks, index):
    rows, width = query_rot.shape
    return pl.pallas_call(
        attend_forward_kernel,
        out_shape=(
            jax.ShapeDtypeStruct((rows, width), jnp.bfloat16),
            jax.ShapeDtypeStruct((rows, width), jnp.float32),
            jax.ShapeDtypeStruct((16, rows), jnp.float32),
        ),
        in_specs=[pl.BlockSpec(memory_space=pltpu.SMEM)] + in_vmem(2),
        out_specs=tuple(in_vmem(3)),
        scratch_shapes=[
            pltpu.VMEM((16, rows), jnp.float32),
            pltpu.VMEM((16, rows), jnp.float32),
            pltpu.VMEM((width, rows), jnp.float32),
        ],
        compiler_params=pltpu.CompilerParams(vmem_limit_bytes=WIDE),
        cost_estimate=pl.CostEstimate(
            flops=16 * rows * rows * width, bytes_accessed=2**22, transcendentals=36 * rows * rows
        ),
    )(index[None], query_rot, blocks)


def attend_backward(query_rot, blocks, grad_heads, attended, log_total, index):
    rows, width = query_rot.shape
    return pl.pallas_call(
        attend_backward_kernel,
        out_shape=(
            jax.ShapeDtypeStruct((rows, width), jnp.float32),
            jax.ShapeDtypeStruct(blocks.shape, jnp.bfloat16),
        ),
        in_specs=[pl.BlockSpec(memory_space=pltpu.SMEM)] + in_vmem(5),
        out_specs=tuple(in_vmem(2)),
        scratch_shapes=[
            pltpu.VMEM((width, rows), jnp.float32),
            pltpu.VMEM((16, rows), jnp.float32),
        ],
        compiler_params=pltpu.CompilerParams(vmem_limit_bytes=WIDE),
        cost_estimate=pl.CostEstimate(
            flops=40 * rows * rows * width, bytes_accessed=2**23, transcendentals=36 * rows * rows
        ),
    )(index[None], query_rot, blocks, grad_heads, attended, log_total)


def forward_attention(block_in, weights, tables, index):
    gain_attn, w_in, w_out, gain_ffn = weights
    tok_count, model_width = block_in.shape
    source = block_in.astype(jnp.float32)
    normed = (source * rms_scale(source) * gain_attn).astype(jnp.bfloat16)
    projected = linear(normed, w_in)
    query_width, key_width = HEADS * HEAD, KV_HEADS * HEAD
    query_rot = (
        rotate(projected[:, :query_width].reshape(1, tok_count, HEADS, HEAD), tables)
        .astype(jnp.bfloat16)
        .reshape(tok_count, query_width)
    )
    key_rot = (
        rotate(
            projected[:, query_width : query_width + key_width].reshape(
                1, tok_count, KV_HEADS, HEAD
            ),
            tables,
        )
        .astype(jnp.bfloat16)
        .reshape(tok_count, key_width)
    )
    values = projected[:, query_width + key_width :].astype(jnp.bfloat16)
    blocks = jnp.stack(gather_xor(jnp.concatenate([key_rot, values], axis=1)))
    return (source, normed, query_rot, blocks)


def forward_rest(source, normed, query_rot, blocks, weights, index):
    gain_attn, w_in, w_out, gain_ffn, w_gate_up, w_down = weights
    mixed_heads, attended, log_total = attend_forward(query_rot, blocks, index)
    hidden = source + linear(mixed_heads, w_out)
    normed_ffn = (hidden * rms_scale(hidden) * gain_ffn).astype(jnp.bfloat16)
    gate_up = linear(normed_ffn, w_gate_up)
    hidden_units = gate_up.shape[1] // 2
    gate_pre, upper = gate_up[:, :hidden_units], gate_up[:, hidden_units:]
    active = (gate_pre * jax.nn.sigmoid(gate_pre) * upper).astype(jnp.bfloat16)
    result = hidden + linear(active, w_down)
    kept = (
        source, normed, query_rot, blocks, log_total, mixed_heads, attended,
        hidden, normed_ffn, gate_up, active,
    )
    return (result, kept)


def backward_ffn(kept, grad_out, weights):
    gain_attn, w_in, w_out, gain_ffn, w_gate_up, w_down = weights
    hidden, normed_ffn, gate_up, active = kept[7:]
    hidden_units = gate_up.shape[1] // 2
    gate_pre, upper = gate_up[:, :hidden_units], gate_up[:, hidden_units:]
    grad_ffn_out = grad_out.astype(jnp.bfloat16)
    grad_active = input_grad(grad_ffn_out, w_down)
    sigmoid_gate = jax.nn.sigmoid(gate_pre)
    grad_gate = (
        grad_active * upper * sigmoid_gate * (1.0 + gate_pre * (1.0 - sigmoid_gate))
    ).astype(jnp.bfloat16)
    grad_upper = (grad_active * gate_pre * sigmoid_gate).astype(jnp.bfloat16)
    grad_both = jnp.concatenate([grad_gate, grad_upper], axis=1)
    g_down = weight_grad(active, grad_ffn_out).astype(jnp.bfloat16)
    g_gate_up = weight_grad(normed_ffn, grad_both).astype(jnp.bfloat16)
    grad_normed_ffn = input_grad(grad_both, w_gate_up)
    grad_part, g_gain_ffn = rms_back(hidden, gain_ffn, grad_normed_ffn)
    return (grad_out + grad_part, g_gain_ffn, g_gate_up, g_down)


def backward_attention(kept, grad_hidden, weights, tables, index, pending=()):
    gain_attn, w_in, w_out, gain_ffn, w_gate_up, w_down = weights
    source, normed, query_rot, blocks, log_total, mixed_heads, attended = kept[:7]
    tok_count = source.shape[0]
    grad_attn = grad_hidden.astype(jnp.bfloat16)
    g_out = weight_grad(mixed_heads, grad_attn)
    grad_heads = input_grad(grad_attn, w_out).astype(jnp.bfloat16)
    grad_query, parts = attend_backward(
        query_rot, blocks, grad_heads, attended, log_total, index
    )
    parts, pending = tied(parts, pending)
    received = xor_send(parts[1::2], "shard", 1)
    own_sum = add_low(parts[0], received[0])
    cross_sum = add_low(parts[2], received[1])
    key_width = KV_HEADS * HEAD
    grad_kv = own_sum.astype(jnp.float32) + xor_send(cross_sum, "shard", 2).astype(jnp.float32)
    grad_query_rows = (
        rotate_back(grad_query.reshape(1, tok_count, HEADS, HEAD), tables)
        .astype(jnp.bfloat16)
        .reshape(tok_count, HEADS * HEAD)
    )
    grad_key_rows = (
        rotate_back(grad_kv[:, :key_width].reshape(1, tok_count, KV_HEADS, HEAD), tables)
        .astype(jnp.bfloat16)
        .reshape(tok_count, key_width)
    )
    grad_rows = jnp.concatenate(
        [grad_query_rows, grad_key_rows, grad_kv[:, key_width:].astype(jnp.bfloat16)], axis=1
    )
    g_in = weight_grad(normed, grad_rows)
    grad_normed = input_grad(grad_rows, w_in)
    grad_part, g_gain_attn = rms_back(source, gain_attn, grad_normed)
    return (grad_hidden + grad_part, g_gain_attn, g_in, g_out, pending)


def both_sections(
    ends, attn_norm, w_query, w_key, w_value, w_out, ffn_norm, w_gate, w_up, w_down
):
    section = lax.axis_index("section")
    leading = section == 0
    index = lax.axis_index("shard")
    replica = lax.axis_index("replica")
    local = ends[0]
    tok_count, model_width = local.shape[-2:]
    own_pair = local.reshape(2, tok_count, model_width)
    moved = fold_rows(
        lax.dynamic_index_in_dim(own_pair, 1 - section, 0, keepdims=False),
        index,
        ((0, 1), (1, 0)),
    )
    stayed = fold_rows(
        lax.dynamic_index_in_dim(own_pair, section, 0, keepdims=False), index, ((0, 0), (1, 1))
    )
    tokens = jnp.where(leading, stayed, moved)
    cotangent = jnp.where(leading, moved, stayed)

    attn_width = w_query.shape[2] + 2 * w_key.shape[2] + w_out.shape[2]
    in_width = attn_width - w_out.shape[2]
    gains = jnp.stack([attn_norm[0], ffn_norm[0]], axis=1)
    groups = (
        jnp.concatenate([w_query[0], w_key[0], w_value[0], w_out[0], gains], axis=1),
        jnp.concatenate([w_gate[0], w_up[0]], axis=1),
        w_down[0],
    )
    chunk = jnp.arange(tok_count // 2, dtype=jnp.int32)
    positions = jnp.concatenate(
        [index * chunk.shape[0] + chunk, (7 - index) * chunk.shape[0] + chunk]
    )
    tables = rotation_tables(positions)
    other_attn = xor_send(groups[0], "section", 1)
    own_rest, other_attn = tied(groups[1:], other_attn)
    other_rest = tuple(xor_send(group, "section", 1) for group in own_rest)

    def of_layer(layer, own, other):
        return jnp.where(section == layer, own, other)

    def attn_weights(layer, own, other):
        attn = gather_rows(of_layer(layer, own, other), index)
        return (
            attn[:, attn_width].astype(jnp.float32),
            attn[:, :in_width],
            attn[:, in_width:attn_width],
            attn[:, attn_width + 1].astype(jnp.float32),
        )

    attn_first = attn_weights(0, groups[0], other_attn)
    first_state = forward_attention(tokens, attn_first, tables, index)
    first_rest, sent_blocks = tied(
        tuple(of_layer(0, own, other) for own, other in zip(own_rest, other_rest)), first_state[3]
    )
    first_state = first_state[:3] + (sent_blocks,)
    first_rest = tuple(gather_rows(group, index) for group in first_rest)
    second_own, second_other, first_rest = tied(groups, (other_attn,) + other_rest, first_rest)
    weights_first = attn_first + first_rest
    attn_second = attn_weights(1, second_own[0], second_other[0])
    middle, kept_first = forward_rest(*first_state, weights_first, index)
    second_state = forward_attention(middle.astype(jnp.bfloat16), attn_second, tables, index)
    second_rest = tuple(
        gather_rows(of_layer(1, own, other), index)
        for own, other in zip(second_own[1:], second_other[1:])
    )
    weights_second = attn_second + second_rest
    final, kept_second = forward_rest(*second_state, weights_second, index)
    final_low = final.astype(jnp.bfloat16)
    final_arrived = unfold_rows(final_low, index, ((0, 1),))
    final_stayed = unfold_rows(final_low, index, ((1, 1),))

    def pack(g_in, g_out, g_gain_attn, g_gain_ffn):
        pad = jnp.zeros((model_width, 2048 - attn_width - 2), jnp.float32)
        parts = [g_in, g_out, g_gain_attn[:, None], g_gain_ffn[:, None], pad]
        return jnp.concatenate([part.astype(jnp.bfloat16) for part in parts], axis=1)

    def over_shards(*partials):
        return tuple(reduce_to_owner(partial, index) for partial in partials)

    def over_replicas(gate_up, down):
        return (reduce_replicas(gate_up, replica, 1), reduce_replicas(down, replica, 0))

    grad_hidden, g_gain_ffn, g_gate_up, g_down = backward_ffn(
        kept_second, cotangent.astype(jnp.float32), weights_second
    )
    ffn_second = over_shards(g_gate_up, g_down)
    grad, g_gain_attn, g_in, g_out, _ = backward_attention(
        kept_second, grad_hidden, weights_second, tables, index
    )
    grad, ffn_second = tied(grad.astype(jnp.bfloat16), ffn_second)
    ffn_second = over_replicas(*ffn_second)
    (attn_second_sum,) = over_shards(pack(g_in, g_out, g_gain_attn, g_gain_ffn))
    grad_hidden, g_gain_ffn, g_gate_up, g_down = backward_ffn(
        kept_first, grad.astype(jnp.float32), weights_first
    )
    grad_hidden, ffn_second, attn_second_sum = tied(grad_hidden, ffn_second, attn_second_sum)
    ffn_second = tuple(reduce_sections(value, 1) for value in ffn_second)
    attn_second_sum = reduce_sections(reduce_replicas(attn_second_sum, replica, 1), 1)
    ffn_first = over_shards(g_gate_up, g_down)
    grad, g_gain_attn, g_in, g_out, (ffn_first, ffn_second, attn_second_sum) = backward_attention(
        kept_first, grad_hidden, weights_first, tables, index,
        (ffn_first, ffn_second, attn_second_sum),
    )
    ffn_first = tuple(reduce_sections(value, 0) for value in over_replicas(*ffn_first))
    (attn_first_sum,) = over_shards(pack(g_in, g_out, g_gain_attn, g_gain_ffn))
    attn_first_sum = reduce_sections(reduce_replicas(attn_first_sum, replica, 1), 0)
    quarters = ((attn_second_sum,) + ffn_second, (attn_first_sum,) + ffn_first)
    grad_low = grad.astype(jnp.bfloat16)
    grad_stayed = unfold_rows(grad_low, index, ((0, 0),))
    grad_arrived = unfold_rows(grad_low, index, ((1, 0),))
    attn_sum, gate_up_sum, down_sum = [
        gather_replicas(jnp.where(leading, first, second), replica, axis).astype(jnp.float32)
        for first, second, axis in zip(quarters[1], quarters[0], (1, 1, 0))
    ]
    ends_out = jnp.stack(
        [
            jnp.where(leading, grad_stayed, final_arrived).astype(jnp.float32),
            jnp.where(leading, grad_arrived, final_stayed).astype(jnp.float32),
        ]
    ).reshape(1, 2, 1, tok_count, model_width)
    cuts = [w_query.shape[2], w_query.shape[2] + w_key.shape[2], in_width, attn_width]
    g_query, g_key, g_value, g_out, _ = jnp.split(attn_sum, cuts, axis=1)
    units = w_gate.shape[2]
    return (
        ends_out,
        attn_sum[:, attn_width][None],
        g_query[None],
        g_key[None],
        g_value[None],
        g_out[None],
        attn_sum[:, attn_width + 1][None],
        gate_up_sum[:, :units][None],
        gate_up_sum[:, units:][None],
        down_sum[None],
    )


def solution(mesh):
    balanced = (
        mesh.shape["section"] == 2 and mesh.shape["replica"] == 4 and mesh.shape["shard"] == 4
    )
    program = both_sections if balanced else on_device
    return jax.shard_map(
        program,
        mesh=mesh,
        in_specs=(
            P("section", None, "replica", "shard", None),
            P("section", "shard"),
            P("section", "shard", None),
            P("section", "shard", None),
            P("section", "shard", None),
            P("section", "shard", None),
            P("section", "shard"),
            P("section", "shard", None),
            P("section", "shard", None),
            P("section", "shard", None),
        ),
        out_specs=(
            P("section", None, "replica", "shard", None),
            P("section", "shard"),
            P("section", "shard", None),
            P("section", "shard", None),
            P("section", "shard", None),
            P("section", "shard", None),
            P("section", "shard"),
            P("section", "shard", None),
            P("section", "shard", None),
            P("section", "shard", None),
        ),
        check_vma=False,
    )
```

```python
from functools import partial

import jax
import jax.numpy as jnp
from jax import lax
from jax.experimental import pallas as pl
from jax.experimental.pallas import tpu as pltpu
from jax.sharding import PartitionSpec as P

HEADS = 9
KV_HEADS = 3
HEAD = 64


epsilon = 1e-05
rope_base = 100000.0
neg_large = -1e30


def shifted(shard, axis, by):
    peers = lax.axis_size(axis)
    pairs = [(i, i + by) for i in range(peers) if 0 <= i + by < peers]
    return lax.ppermute(shard, axis, pairs)


def rms_scale(source):
    return lax.rsqrt(jnp.mean(source * source, axis=-1, keepdims=True) + epsilon)


def rms_back(source, gain_vector, grad_normed):
    inv_scale = rms_scale(source)
    unit_rows = source * inv_scale
    grad_unit = grad_normed * gain_vector
    gain_grad = jnp.sum(grad_normed * unit_rows, axis=0)
    grad_source = inv_scale * (
        grad_unit - unit_rows * jnp.mean(grad_unit * unit_rows, axis=-1, keepdims=True)
    )
    return (grad_source, gain_grad)


def rotation_tables(positions):
    half_size = HEAD // 2
    frequency = rope_base ** (-jnp.arange(half_size, dtype=jnp.float32) * 2.0 / HEAD)
    angles = positions.astype(jnp.float32)[:, None] * frequency[None, :]
    return (jnp.cos(angles)[None, :, None, :], jnp.sin(angles)[None, :, None, :])


def rotate(tensor, tables):
    cosine, sine_part = tables
    half_size = tensor.shape[-1] // 2
    first_half = tensor[..., :half_size]
    second_half = tensor[..., half_size:]
    return jnp.concatenate(
        [
            first_half * cosine - second_half * sine_part,
            second_half * cosine + first_half * sine_part,
        ],
        axis=-1,
    )


def rotate_back(gradient, tables):
    cosine, sine_part = tables
    half_size = gradient.shape[-1] // 2
    first_half = gradient[..., :half_size]
    second_half = gradient[..., half_size:]
    return jnp.concatenate(
        [
            first_half * cosine + second_half * sine_part,
            second_half * cosine - first_half * sine_part,
        ],
        axis=-1,
    )


def linear(left_side, right_side):
    return jnp.dot(left_side, right_side, preferred_element_type=jnp.float32)


def weight_grad(left_side, right_side):
    return jnp.einsum("rd,rf->df", left_side, right_side, preferred_element_type=jnp.float32)


def input_grad(gradient, weight):
    return jnp.einsum("rf,df->rd", gradient, weight, preferred_element_type=jnp.float32)


def split_blocks(tensor):
    seq_count, length, head_count, head_size = tensor.shape
    block_rows = min(512, length)
    shaped = tensor.reshape(seq_count, length // block_rows, block_rows, head_count, head_size)
    return (jnp.moveaxis(shaped, 1, 0), block_rows)


def block_scores(grouped, key_block, block_start, positions):
    raw_scores = jnp.einsum(
        "stkgd,sukd->skgtu", grouped, key_block, preferred_element_type=jnp.float32
    )
    key_pos = block_start + jnp.arange(key_block.shape[1], dtype=jnp.int32)
    allowed = key_pos[None, :] <= positions[:, None]
    return (jnp.where(allowed, raw_scores * HEAD ** (-0.5), neg_large), allowed)


def keep_carry(state_triple):
    return state_triple


def scatter_at_end(parts):
    attn_shares = (
        lax.psum_scatter(
            parts[0].astype(jnp.bfloat16), "shard", scatter_dimension=0, tiled=True
        ).astype(jnp.float32),
        lax.psum_scatter(
            parts[1].astype(jnp.bfloat16), "shard", scatter_dimension=0, tiled=True
        ).astype(jnp.float32),
        lax.psum_scatter(
            parts[2].astype(jnp.bfloat16), "shard", scatter_dimension=0, tiled=True
        ).astype(jnp.float32),
        lax.psum_scatter(
            parts[3].astype(jnp.bfloat16), "shard", scatter_dimension=0, tiled=True
        ).astype(jnp.float32),
        lax.psum_scatter(
            parts[4].astype(jnp.bfloat16), "shard", scatter_dimension=0, tiled=True
        ).astype(jnp.float32),
        lax.psum_scatter(
            parts[5].astype(jnp.bfloat16), "shard", scatter_dimension=0, tiled=True
        ).astype(jnp.float32),
    )
    ffn_shares = (
        lax.psum_scatter(
            parts[6].astype(jnp.bfloat16), "shard", scatter_dimension=0, tiled=True
        ).astype(jnp.float32),
        lax.psum_scatter(
            parts[7].astype(jnp.bfloat16), "shard", scatter_dimension=0, tiled=True
        ).astype(jnp.float32),
    )
    down_share = lax.psum_scatter(
        parts[8].astype(jnp.bfloat16), "shard", scatter_dimension=0, tiled=True
    ).astype(jnp.float32)
    return tuple(attn_shares) + tuple(ffn_shares) + (down_share,)


def forward_layer(block_in, weights, tables, positions):
    gain_attn, w_query, w_key, w_value, w_out, gain_ffn, w_gate, w_up, w_down = weights
    seq_count, tok_count, model_width = block_in.shape
    group_size = HEADS // KV_HEADS
    source = block_in.astype(jnp.float32).reshape(seq_count * tok_count, model_width)
    normed = (source * rms_scale(source) * gain_attn.astype(jnp.float32)).astype(jnp.bfloat16)
    query_rot = rotate(
        linear(normed, w_query).reshape(seq_count, tok_count, HEADS, HEAD), tables
    ).astype(jnp.bfloat16)
    key_rot = rotate(
        linear(normed, w_key).reshape(seq_count, tok_count, KV_HEADS, HEAD), tables
    ).astype(jnp.bfloat16)
    values = (
        linear(normed, w_value).astype(jnp.bfloat16).reshape(seq_count, tok_count, KV_HEADS, HEAD)
    )
    keys_all, values_all = (
        lax.all_gather(key_rot, "shard", axis=1, tiled=True),
        lax.all_gather(values, "shard", axis=1, tiled=True),
    )
    grouped = query_rot.reshape(seq_count, tok_count, KV_HEADS, group_size, HEAD)
    key_blocks, block_rows = split_blocks(keys_all)
    value_blocks, block_rows = split_blocks(values_all)
    block_ids = jnp.arange(key_blocks.shape[0], dtype=jnp.int32)
    last_query = positions[-1]

    def attend_step(state_triple, block_args):
        key_block, value_block, block_index = block_args
        block_start = block_index * block_rows

        def attend_update(state_triple):
            running_top, running_sum, mixed_sum = state_triple
            scores, allowed = block_scores(grouped, key_block, block_start, positions)
            new_top = jnp.maximum(running_top, jnp.max(scores, axis=-1))
            weights_now = jnp.where(allowed, jnp.exp(scores - new_top[..., None]), 0.0)
            factor = jnp.exp(running_top - new_top)
            running_sum = running_sum * factor + jnp.sum(weights_now, axis=-1)
            mixed_sum = mixed_sum * jnp.moveaxis(factor, 3, 1)[..., None] + jnp.einsum(
                "skgtu,sukd->stkgd",
                weights_now.astype(jnp.bfloat16),
                value_block,
                preferred_element_type=jnp.float32,
            )
            return (new_top, running_sum, mixed_sum)

        return (lax.cond(block_start <= last_query, attend_update, keep_carry, state_triple), None)

    stats_shape = (seq_count, KV_HEADS, group_size, tok_count)
    start_triple = (
        jnp.full(stats_shape, neg_large, jnp.float32),
        jnp.zeros(stats_shape, jnp.float32),
        jnp.zeros(grouped.shape, jnp.float32),
    )
    (running_top, running_sum, mixed_sum), unused = lax.scan(
        attend_step, start_triple, (key_blocks, value_blocks, block_ids)
    )
    log_total = running_top + jnp.log(running_sum)
    attended = mixed_sum / jnp.moveaxis(running_sum, 3, 1)[..., None]
    mixed_heads = attended.astype(jnp.bfloat16).reshape(seq_count * tok_count, HEADS * HEAD)
    hidden = source + linear(mixed_heads, w_out)
    normed_ffn = (hidden * rms_scale(hidden) * gain_ffn.astype(jnp.float32)).astype(jnp.bfloat16)
    gate_pre = linear(normed_ffn, w_gate)
    upper = linear(normed_ffn, w_up)
    active = (gate_pre * jax.nn.sigmoid(gate_pre) * upper).astype(jnp.bfloat16)
    result = hidden + linear(active, w_down)
    kept_state = (
        block_in,
        normed,
        grouped,
        key_blocks,
        value_blocks,
        log_total,
        mixed_heads,
        attended,
        hidden,
        normed_ffn,
        gate_pre,
        upper,
        active,
    )
    return (result, kept_state)


def backward_layer(kept_state, grad_out, weights, tables, positions):
    gain_attn, w_query, w_key, w_value, w_out, gain_ffn, w_gate, w_up, w_down = weights
    (
        block_in,
        normed,
        grouped,
        key_blocks,
        value_blocks,
        log_total,
        mixed_heads,
        attended,
        hidden,
        normed_ffn,
        gate_pre,
        upper,
        active,
    ) = kept_state
    seq_count, tok_count, model_width = block_in.shape
    block_rows = key_blocks.shape[2]
    source = block_in.astype(jnp.float32).reshape(seq_count * tok_count, model_width)
    grad_ffn_out = grad_out.astype(jnp.bfloat16)
    g_down = weight_grad(active, grad_ffn_out)
    grad_active = input_grad(grad_ffn_out, w_down)
    sigmoid_gate = jax.nn.sigmoid(gate_pre)
    grad_gate = (
        grad_active * upper * sigmoid_gate * (1.0 + gate_pre * (1.0 - sigmoid_gate))
    ).astype(jnp.bfloat16)
    grad_upper = (grad_active * gate_pre * sigmoid_gate).astype(jnp.bfloat16)
    g_gate = weight_grad(normed_ffn, grad_gate)
    g_up = weight_grad(normed_ffn, grad_upper)
    grad_normed_ffn = input_grad(grad_gate, w_gate) + input_grad(grad_upper, w_up)
    grad_hidden_part, g_gain_ffn = rms_back(hidden, gain_ffn.astype(jnp.float32), grad_normed_ffn)
    grad_hidden = grad_out + grad_hidden_part
    grad_attn = grad_hidden.astype(jnp.bfloat16)
    g_out = weight_grad(mixed_heads, grad_attn)
    grad_heads = input_grad(grad_attn, w_out).astype(jnp.bfloat16).reshape(grouped.shape)
    row_delta = jnp.moveaxis(jnp.sum(grad_heads.astype(jnp.float32) * attended, axis=-1), 1, 3)
    block_ids = jnp.arange(key_blocks.shape[0], dtype=jnp.int32)
    last_query = positions[-1]

    def grad_step(grad_query, block_args):
        key_block, value_block, block_index = block_args
        block_start = block_index * block_rows

        def grad_update(grad_query):
            scores, allowed = block_scores(grouped, key_block, block_start, positions)
            probabilities = jnp.where(allowed, jnp.exp(scores - log_total[..., None]), 0.0)
            grad_probs = jnp.einsum(
                "stkgd,sukd->skgtu", grad_heads, value_block, preferred_element_type=jnp.float32
            )
            grad_scores = (
                probabilities * (grad_probs - row_delta[..., None]) * HEAD ** (-0.5)
            ).astype(jnp.bfloat16)
            grad_query = grad_query + jnp.einsum(
                "skgtu,sukd->stkgd", grad_scores, key_block, preferred_element_type=jnp.float32
            )
            grad_key_block = jnp.einsum(
                "skgtu,stkgd->sukd", grad_scores, grouped, preferred_element_type=jnp.float32
            )
            grad_value_block = jnp.einsum(
                "skgtu,stkgd->sukd",
                probabilities.astype(jnp.bfloat16),
                grad_heads,
                preferred_element_type=jnp.float32,
            )
            return (grad_query, (grad_key_block, grad_value_block))

        def skip_block(grad_query):
            empty_grad = jnp.zeros(key_block.shape, jnp.float32)
            return (grad_query, (empty_grad, empty_grad))

        return lax.cond(block_start <= last_query, grad_update, skip_block, grad_query)

    grad_query, (key_parts, value_parts) = lax.scan(
        grad_step, jnp.zeros(grouped.shape, jnp.float32), (key_blocks, value_blocks, block_ids)
    )
    full_shape = (seq_count, key_parts.shape[0] * block_rows, KV_HEADS, HEAD)
    key_full = jnp.moveaxis(key_parts, 0, 1).reshape(full_shape)
    value_full = jnp.moveaxis(value_parts, 0, 1).reshape(full_shape)
    grad_keys, grad_values = (
        lax.psum_scatter(
            key_full.astype(jnp.bfloat16), "shard", scatter_dimension=1, tiled=True
        ).astype(jnp.float32),
        lax.psum_scatter(
            value_full.astype(jnp.bfloat16), "shard", scatter_dimension=1, tiled=True
        ).astype(jnp.float32),
    )
    row_count = seq_count * tok_count
    grad_query_rows = (
        rotate_back(grad_query.reshape(seq_count, tok_count, HEADS, HEAD), tables)
        .astype(jnp.bfloat16)
        .reshape(row_count, HEADS * HEAD)
    )
    grad_key_rows = (
        rotate_back(grad_keys, tables).astype(jnp.bfloat16).reshape(row_count, KV_HEADS * HEAD)
    )
    grad_value_rows = grad_values.astype(jnp.bfloat16).reshape(row_count, KV_HEADS * HEAD)
    g_query = weight_grad(normed, grad_query_rows)
    g_key = weight_grad(normed, grad_key_rows)
    g_value = weight_grad(normed, grad_value_rows)
    grad_normed = (
        input_grad(grad_query_rows, w_query)
        + input_grad(grad_key_rows, w_key)
        + input_grad(grad_value_rows, w_value)
    )
    grad_source_part, g_gain_attn = rms_back(source, gain_attn.astype(jnp.float32), grad_normed)
    grad_source = grad_hidden + grad_source_part
    return (
        grad_source,
        (g_gain_attn, g_query, g_key, g_value, g_out, g_gain_ffn, g_gate, g_up, g_down),
    )


def on_device(ends, attn_norm, w_query, w_key, w_value, w_out, ffn_norm, w_gate, w_up, w_down):
    params = (
        attn_norm[0],
        w_query[0],
        w_key[0],
        w_value[0],
        w_out[0],
        ffn_norm[0],
        w_gate[0],
        w_up[0],
        w_down[0],
    )
    leading = lax.axis_index("section") == 0
    held_weights = (
        lax.all_gather(params[0], "shard", axis=0, tiled=True),
        lax.all_gather(params[1], "shard", axis=0, tiled=True),
        lax.all_gather(params[2], "shard", axis=0, tiled=True),
        lax.all_gather(params[3], "shard", axis=0, tiled=True),
        lax.all_gather(params[4], "shard", axis=0, tiled=True),
        lax.all_gather(params[5], "shard", axis=0, tiled=True),
        lax.all_gather(params[6], "shard", axis=0, tiled=True),
        lax.all_gather(params[7], "shard", axis=0, tiled=True),
        lax.all_gather(params[8], "shard", axis=0, tiled=True),
    )
    local_ends = ends[0]
    micro_count, seq_count, tok_count, model_width = local_ends.shape
    positions = lax.axis_index("shard") * tok_count + jnp.arange(tok_count, dtype=jnp.int32)
    tables = rotation_tables(positions)
    arriving = jnp.zeros((seq_count, tok_count, model_width), jnp.bfloat16)
    kept_states = []
    layer_outputs = []
    for moment in range(micro_count + 1):
        own_rows = local_ends[moment] if moment < micro_count else jnp.zeros_like(arriving)
        block_in = jnp.where(leading, own_rows, arriving)
        result, kept_state = forward_layer(block_in, held_weights, tables, positions)
        kept_states.append(kept_state)
        if moment > 0:
            layer_outputs.append(result)
        if moment < micro_count:
            arriving = shifted(
                result.astype(jnp.bfloat16).reshape(seq_count, tok_count, model_width), "section", 1
            )
    returning = jnp.zeros((seq_count * tok_count, model_width), jnp.float32)
    totals = None
    input_grads = []
    for moment in range(micro_count + 1):
        earlier = moment - 1 if moment > 0 else micro_count
        later = moment + 1 if moment < micro_count else 0
        kept_state = jax.tree.map(
            partial(jnp.where, leading), kept_states[earlier], kept_states[later]
        )
        if moment < micro_count:
            own_grad = (
                local_ends[moment].astype(jnp.float32).reshape(seq_count * tok_count, model_width)
            )
        else:
            own_grad = jnp.zeros_like(returning)
        grad_source, grad_parts = backward_layer(
            kept_state, jnp.where(leading, returning, own_grad), held_weights, tables, positions
        )
        totals = grad_parts if totals is None else jax.tree.map(jnp.add, totals, grad_parts)
        if moment > 0:
            input_grads.append(grad_source)
        if moment < micro_count:
            returning = shifted(grad_source.astype(jnp.bfloat16), "section", -1).astype(jnp.float32)
    pieces = [
        jnp.where(leading, input_grads[number], layer_outputs[number])
        for number in range(micro_count)
    ]
    ends_out = jnp.stack(pieces).reshape(1, micro_count, seq_count, tok_count, model_width)
    shares = scatter_at_end(totals)
    summed = (
        lax.psum(shares[0].astype(jnp.bfloat16), "replica").astype(jnp.float32),
        lax.psum(shares[1].astype(jnp.bfloat16), "replica").astype(jnp.float32),
        lax.psum(shares[2].astype(jnp.bfloat16), "replica").astype(jnp.float32),
        lax.psum(shares[3].astype(jnp.bfloat16), "replica").astype(jnp.float32),
        lax.psum(shares[4].astype(jnp.bfloat16), "replica").astype(jnp.float32),
        lax.psum(shares[5].astype(jnp.bfloat16), "replica").astype(jnp.float32),
        lax.psum(shares[6].astype(jnp.bfloat16), "replica").astype(jnp.float32),
        lax.psum(shares[7].astype(jnp.bfloat16), "replica").astype(jnp.float32),
        lax.psum(shares[8].astype(jnp.bfloat16), "replica").astype(jnp.float32),
    )
    return (ends_out,) + tuple((share[None] for share in summed))


def xor_send(value, axis, bits):
    peers = lax.axis_size(axis)
    return lax.ppermute(value, axis, [(i, i ^ bits) for i in range(peers)])


def xor_sort(parts, index):
    low_bit, high_bit = (index & 1) == 1, (index & 2) == 2
    a, b, c, d = parts
    pairs = (
        jnp.where(low_bit, b, a),
        jnp.where(low_bit, a, b),
        jnp.where(low_bit, d, c),
        jnp.where(low_bit, c, d),
    )
    return (
        jnp.where(high_bit, pairs[2], pairs[0]),
        jnp.where(high_bit, pairs[3], pairs[1]),
        jnp.where(high_bit, pairs[0], pairs[2]),
        jnp.where(high_bit, pairs[1], pairs[3]),
    )


def gather_xor(value):
    crossed = xor_send(value, "shard", 2)
    beside = xor_send(value, "shard", 1)
    far = xor_send(crossed, "shard", 1)
    return (value, beside, crossed, far)


def gather_rows(value, index):
    return jnp.concatenate(xor_sort(gather_xor(value), index), axis=0)


def add_low(first, second):
    return (first.astype(jnp.float32) + second.astype(jnp.float32)).astype(jnp.bfloat16)


def reduce_to_owner(partial, index):
    rows = partial.shape[0] // 4
    core, chip = index & 1, index >> 1

    def block(number):
        return lax.dynamic_slice_in_dim(partial, number * rows, rows, 0)

    far, near = [
        add_low(block(2 * owner + core), xor_send(block(2 * owner + (core ^ 1)), "shard", 1))
        for owner in (chip ^ 1, chip)
    ]
    return add_low(near, xor_send(far, "shard", 2))


FOLD = ((0, 2, 3, 1), (1, 3, 2, 0))


def section_pairs(half, moves, back):
    pairs = []
    for start, end in moves:
        for held, folded in enumerate(FOLD[half]):
            ends = (start * 4 + held, end * 4 + folded)
            if back:
                ends = (start * 4 + folded, end * 4 + held)
            pairs.append(ends)
    return pairs


def fold_rows(rows, index, moves):
    size = rows.shape[0] // 2
    first, second = [
        lax.ppermute(
            rows[half * size : (half + 1) * size],
            ("section", "shard"),
            section_pairs(half, moves, False),
        )
        for half in (0, 1)
    ]
    odd = (index & 1) == 1
    return jnp.concatenate([jnp.where(odd, second, first), jnp.where(odd, first, second)], axis=0)


def unfold_rows(rows, index, moves):
    size = rows.shape[0] // 2
    low, high = rows[:size], rows[size:]
    odd = (index & 1) == 1
    parts = (jnp.where(odd, high, low), jnp.where(odd, low, high))
    return jnp.concatenate(
        [
            lax.ppermute(parts[half], ("section", "shard"), section_pairs(half, moves, True))
            for half in (0, 1)
        ],
        axis=0,
    )


def reduce_replicas(value, replica, axis):
    size = value.shape[axis] // 4

    def quarter(number):
        return lax.dynamic_slice_in_dim(value, number * size, size, axis)

    total = quarter(replica).astype(jnp.float32)
    for bits in (1, 2, 3):
        total = total + xor_send(quarter(replica ^ bits), "replica", bits).astype(jnp.float32)
    return total.astype(jnp.bfloat16)


def gather_replicas(value, replica, axis):
    parts = (value,) + tuple(xor_send(value, "replica", bits) for bits in (1, 2, 3))
    return jnp.concatenate(xor_sort(parts, replica), axis=axis)


def reduce_sections(value, layer):
    return add_low(value, lax.ppermute(value, "section", [(1 - layer, layer)]))


def tied(*values):
    return lax.optimization_barrier(values)


WIDE = 50 * 2**20


def nt_dot(left, right):
    return lax.dot_general(left, right, (((1,), (1,)), ((), ())), preferred_element_type=jnp.float32)


def tn_dot(left, right):
    return lax.dot_general(left, right, (((0,), (0,)), ((), ())), preferred_element_type=jnp.float32)


def head_columns(head, start=0):
    return slice(start + head * HEAD, start + (head + 1) * HEAD)


def over_blocks(index, rows, update):
    every, early, late = slice(0, rows), slice(0, rows // 2), slice(rows // 2, rows)
    update(0, True, every, every)

    def other(j, carry):
        before = (index ^ j) < index

        @pl.when(before)
        def _():
            update(j, False, early, every)

        @pl.when(jnp.logical_not(before))
        def _():
            update(j, False, every, late)

        return carry

    lax.fori_loop(1, 4, other, 0)


def causal(rows):
    keys = lax.broadcasted_iota(jnp.int32, (rows, rows), 0)
    queries = lax.broadcasted_iota(jnp.int32, (rows, rows), 1)
    return keys <= queries


def attend_forward_kernel(index_ref, q_ref, blocks_ref, mixed_ref, attended_ref, log_ref, top, total, acc):
    rows = q_ref.shape[0]
    group = HEADS // KV_HEADS

    def update(j, own, met, asked):
        for kv in range(KV_HEADS):
            keys = blocks_ref[j, met, head_columns(kv)]
            values = blocks_ref[j, met, head_columns(kv, KV_HEADS * HEAD)]
            for head in range(kv * group, (kv + 1) * group):
                line = slice(head, head + 1)
                scores = nt_dot(keys, q_ref[asked, head_columns(head)] * HEAD ** (-0.5))
                if own:
                    scores = jnp.where(causal(rows), scores, neg_large)
                    new_top = jnp.max(scores, axis=0, keepdims=True)
                else:
                    new_top = jnp.maximum(top[line, asked], jnp.max(scores, axis=0, keepdims=True))
                weights_now = jnp.exp(scores - new_top)
                sums = jnp.sum(weights_now, axis=0, keepdims=True)
                mixed = tn_dot(values, weights_now.astype(jnp.bfloat16))
                if not own:
                    factor = jnp.exp(top[line, asked] - new_top)
                    sums = sums + total[line, asked] * factor
                    mixed = mixed + acc[head_columns(head), asked] * factor
                top[line, asked] = new_top
                total[line, asked] = sums
                acc[head_columns(head), asked] = mixed

    over_blocks(index_ref[0], rows, update)
    log_ref[...] = jnp.zeros_like(log_ref)
    for head in range(HEADS):
        line = slice(head, head + 1)
        log_ref[line, :] = top[line, :] + jnp.log(total[line, :])
        acc[head_columns(head), :] = acc[head_columns(head), :] / total[line, :]
    attended = acc[...].T
    attended_ref[...] = attended
    mixed_ref[...] = attended.astype(jnp.bfloat16)


def attend_backward_kernel(
    index_ref, q_ref, blocks_ref, grads_ref, attended_ref, log_ref, query_ref, parts_ref, acc, delta
):
    rows = q_ref.shape[0]
    group = HEADS // KV_HEADS
    width = KV_HEADS * HEAD
    parts_ref[...] = jnp.zeros_like(parts_ref)
    acc[...] = (grads_ref[...].astype(jnp.float32) * attended_ref[...]).T
    for head in range(HEADS):
        delta[head : head + 1, :] = jnp.sum(acc[head_columns(head), :], axis=0, keepdims=True)
    acc[...] = jnp.zeros_like(acc)

    def update(j, own, met, asked):
        for kv in range(KV_HEADS):
            keys = blocks_ref[j, met, head_columns(kv)]
            values = blocks_ref[j, met, head_columns(kv, width)]
            key_sum = jnp.zeros((met.stop - met.start, HEAD), jnp.float32)
            value_sum = jnp.zeros((met.stop - met.start, HEAD), jnp.float32)
            for head in range(kv * group, (kv + 1) * group):
                line = slice(head, head + 1)
                query = q_ref[asked, head_columns(head)]
                grads = grads_ref[asked, head_columns(head)]
                scores = nt_dot(keys, query * HEAD ** (-0.5))
                if own:
                    scores = jnp.where(causal(rows), scores, neg_large)
                probabilities = jnp.exp(scores - log_ref[line, asked])
                grad_probs = nt_dot(values, grads)
                grad_scores = (
                    probabilities * (grad_probs - delta[line, asked]) * HEAD ** (-0.5)
                ).astype(jnp.bfloat16)
                acc[head_columns(head), asked] += tn_dot(keys, grad_scores)
                key_sum += jnp.dot(grad_scores, query, preferred_element_type=jnp.float32)
                value_sum += jnp.dot(
                    probabilities.astype(jnp.bfloat16), grads, preferred_element_type=jnp.float32
                )
            parts_ref[j, met, head_columns(kv)] = key_sum.astype(jnp.bfloat16)
            parts_ref[j, met, head_columns(kv, width)] = value_sum.astype(jnp.bfloat16)

    over_blocks(index_ref[0], rows, update)
    query_ref[...] = acc[...].T


def in_vmem(count):
    return [pl.BlockSpec(memory_space=pltpu.VMEM)] * count


def attend_forward(query_rot, blocks, index):
    rows, width = query_rot.shape
    return pl.pallas_call(
        attend_forward_kernel,
        out_shape=(
            jax.ShapeDtypeStruct((rows, width), jnp.bfloat16),
            jax.ShapeDtypeStruct((rows, width), jnp.float32),
            jax.ShapeDtypeStruct((16, rows), jnp.float32),
        ),
        in_specs=[pl.BlockSpec(memory_space=pltpu.SMEM)] + in_vmem(2),
        out_specs=tuple(in_vmem(3)),
        scratch_shapes=[
            pltpu.VMEM((16, rows), jnp.float32),
            pltpu.VMEM((16, rows), jnp.float32),
            pltpu.VMEM((width, rows), jnp.float32),
        ],
        compiler_params=pltpu.CompilerParams(vmem_limit_bytes=WIDE),
        cost_estimate=pl.CostEstimate(
            flops=16 * rows * rows * width, bytes_accessed=2**22, transcendentals=36 * rows * rows
        ),
    )(index[None], query_rot, blocks)


def attend_backward(query_rot, blocks, grad_heads, attended, log_total, index):
    rows, width = query_rot.shape
    return pl.pallas_call(
        attend_backward_kernel,
        out_shape=(
            jax.ShapeDtypeStruct((rows, width), jnp.float32),
            jax.ShapeDtypeStruct(blocks.shape, jnp.bfloat16),
        ),
        in_specs=[pl.BlockSpec(memory_space=pltpu.SMEM)] + in_vmem(5),
        out_specs=tuple(in_vmem(2)),
        scratch_shapes=[
            pltpu.VMEM((width, rows), jnp.float32),
            pltpu.VMEM((16, rows), jnp.float32),
        ],
        compiler_params=pltpu.CompilerParams(vmem_limit_bytes=WIDE),
        cost_estimate=pl.CostEstimate(
            flops=40 * rows * rows * width, bytes_accessed=2**23, transcendentals=36 * rows * rows
        ),
    )(index[None], query_rot, blocks, grad_heads, attended, log_total)


def forward_attention(block_in, weights, tables, index):
    gain_attn, w_in, w_out, gain_ffn = weights
    tok_count, model_width = block_in.shape
    source = block_in.astype(jnp.float32)
    normed = (source * rms_scale(source) * gain_attn).astype(jnp.bfloat16)
    projected = linear(normed, w_in)
    query_width, key_width = HEADS * HEAD, KV_HEADS * HEAD
    query_rot = (
        rotate(projected[:, :query_width].reshape(1, tok_count, HEADS, HEAD), tables)
        .astype(jnp.bfloat16)
        .reshape(tok_count, query_width)
    )
    key_rot = (
        rotate(
            projected[:, query_width : query_width + key_width].reshape(
                1, tok_count, KV_HEADS, HEAD
            ),
            tables,
        )
        .astype(jnp.bfloat16)
        .reshape(tok_count, key_width)
    )
    values = projected[:, query_width + key_width :].astype(jnp.bfloat16)
    blocks = jnp.stack(gather_xor(jnp.concatenate([key_rot, values], axis=1)))
    return (source, normed, query_rot, blocks)


def forward_rest(source, normed, query_rot, blocks, weights, index):
    gain_attn, w_in, w_out, gain_ffn, w_gate_up, w_down = weights
    mixed_heads, attended, log_total = attend_forward(query_rot, blocks, index)
    hidden = source + linear(mixed_heads, w_out)
    normed_ffn = (hidden * rms_scale(hidden) * gain_ffn).astype(jnp.bfloat16)
    gate_up = linear(normed_ffn, w_gate_up)
    hidden_units = gate_up.shape[1] // 2
    gate_pre, upper = gate_up[:, :hidden_units], gate_up[:, hidden_units:]
    active = (gate_pre * jax.nn.sigmoid(gate_pre) * upper).astype(jnp.bfloat16)
    result = hidden + linear(active, w_down)
    kept = (
        source, normed, query_rot, blocks, log_total, mixed_heads, attended,
        hidden, normed_ffn, gate_up, active,
    )
    return (result, kept)


def backward_ffn(kept, grad_out, weights):
    gain_attn, w_in, w_out, gain_ffn, w_gate_up, w_down = weights
    hidden, normed_ffn, gate_up, active = kept[7:]
    hidden_units = gate_up.shape[1] // 2
    gate_pre, upper = gate_up[:, :hidden_units], gate_up[:, hidden_units:]
    grad_ffn_out = grad_out.astype(jnp.bfloat16)
    grad_active = input_grad(grad_ffn_out, w_down)
    sigmoid_gate = jax.nn.sigmoid(gate_pre)
    grad_gate = (
        grad_active * upper * sigmoid_gate * (1.0 + gate_pre * (1.0 - sigmoid_gate))
    ).astype(jnp.bfloat16)
    grad_upper = (grad_active * gate_pre * sigmoid_gate).astype(jnp.bfloat16)
    grad_both = jnp.concatenate([grad_gate, grad_upper], axis=1)
    g_down = weight_grad(active, grad_ffn_out).astype(jnp.bfloat16)
    g_gate_up = weight_grad(normed_ffn, grad_both).astype(jnp.bfloat16)
    grad_normed_ffn = input_grad(grad_both, w_gate_up)
    grad_part, g_gain_ffn = rms_back(hidden, gain_ffn, grad_normed_ffn)
    return (grad_out + grad_part, g_gain_ffn, g_gate_up, g_down)


def backward_attention(kept, grad_hidden, weights, tables, index, pending=()):
    gain_attn, w_in, w_out, gain_ffn, w_gate_up, w_down = weights
    source, normed, query_rot, blocks, log_total, mixed_heads, attended = kept[:7]
    tok_count = source.shape[0]
    grad_attn = grad_hidden.astype(jnp.bfloat16)
    g_out = weight_grad(mixed_heads, grad_attn)
    grad_heads = input_grad(grad_attn, w_out).astype(jnp.bfloat16)
    grad_query, parts = attend_backward(
        query_rot, blocks, grad_heads, attended, log_total, index
    )
    received = xor_send(parts[1::2], "shard", 1)
    own_sum = add_low(parts[0], received[0])
    cross_sum = add_low(parts[2], received[1])
    key_width = KV_HEADS * HEAD
    grad_kv = own_sum.astype(jnp.float32) + xor_send(cross_sum, "shard", 2).astype(jnp.float32)
    grad_kv, pending = tied(grad_kv, pending)
    grad_query_rows = (
        rotate_back(grad_query.reshape(1, tok_count, HEADS, HEAD), tables)
        .astype(jnp.bfloat16)
        .reshape(tok_count, HEADS * HEAD)
    )
    grad_key_rows = (
        rotate_back(grad_kv[:, :key_width].reshape(1, tok_count, KV_HEADS, HEAD), tables)
        .astype(jnp.bfloat16)
        .reshape(tok_count, key_width)
    )
    grad_rows = jnp.concatenate(
        [grad_query_rows, grad_key_rows, grad_kv[:, key_width:].astype(jnp.bfloat16)], axis=1
    )
    g_in = weight_grad(normed, grad_rows)
    grad_normed = input_grad(grad_rows, w_in)
    grad_part, g_gain_attn = rms_back(source, gain_attn, grad_normed)
    return (grad_hidden + grad_part, g_gain_attn, g_in, g_out, pending)


def both_sections(
    ends, attn_norm, w_query, w_key, w_value, w_out, ffn_norm, w_gate, w_up, w_down
):
    section = lax.axis_index("section")
    leading = section == 0
    index = lax.axis_index("shard")
    replica = lax.axis_index("replica")
    local = ends[0]
    tok_count, model_width = local.shape[-2:]
    own_pair = local.reshape(2, tok_count, model_width)
    moved = fold_rows(
        lax.dynamic_index_in_dim(own_pair, 1 - section, 0, keepdims=False),
        index,
        ((0, 1), (1, 0)),
    )
    stayed = fold_rows(
        lax.dynamic_index_in_dim(own_pair, section, 0, keepdims=False), index, ((0, 0), (1, 1))
    )
    tokens = jnp.where(leading, stayed, moved)
    cotangent = jnp.where(leading, moved, stayed)

    attn_width = w_query.shape[2] + 2 * w_key.shape[2] + w_out.shape[2]
    in_width = attn_width - w_out.shape[2]
    gains = jnp.stack([attn_norm[0], ffn_norm[0]], axis=1)
    groups = (
        jnp.concatenate([w_query[0], w_key[0], w_value[0], w_out[0], gains], axis=1),
        jnp.concatenate([w_gate[0], w_up[0]], axis=1),
        w_down[0],
    )
    chunk = jnp.arange(tok_count // 2, dtype=jnp.int32)
    positions = jnp.concatenate(
        [index * chunk.shape[0] + chunk, (7 - index) * chunk.shape[0] + chunk]
    )
    tables = rotation_tables(positions)
    other_attn = xor_send(groups[0], "section", 1)
    own_rest, other_attn = tied(groups[1:], other_attn)
    other_rest = tuple(xor_send(group, "section", 1) for group in own_rest)

    def of_layer(layer, own, other):
        return jnp.where(section == layer, own, other)

    def attn_weights(layer, own, other):
        attn = gather_rows(of_layer(layer, own, other), index)
        return (
            attn[:, attn_width].astype(jnp.float32),
            attn[:, :in_width],
            attn[:, in_width:attn_width],
            attn[:, attn_width + 1].astype(jnp.float32),
        )

    attn_first = attn_weights(0, groups[0], other_attn)
    first_state = forward_attention(tokens, attn_first, tables, index)
    first_rest, sent_blocks = tied(
        tuple(of_layer(0, own, other) for own, other in zip(own_rest, other_rest)), first_state[3]
    )
    first_state = first_state[:3] + (sent_blocks,)
    first_rest = tuple(gather_rows(group, index) for group in first_rest)
    second_own, second_other, first_rest = tied(groups, (other_attn,) + other_rest, first_rest)
    weights_first = attn_first + first_rest
    attn_second = attn_weights(1, second_own[0], second_other[0])
    middle, kept_first = forward_rest(*first_state, weights_first, index)
    second_state = forward_attention(middle.astype(jnp.bfloat16), attn_second, tables, index)
    second_rest = tuple(
        gather_rows(of_layer(1, own, other), index)
        for own, other in zip(second_own[1:], second_other[1:])
    )
    weights_second = attn_second + second_rest
    final, kept_second = forward_rest(*second_state, weights_second, index)
    final_low = final.astype(jnp.bfloat16)
    final_arrived = unfold_rows(final_low, index, ((0, 1),))
    final_stayed = unfold_rows(final_low, index, ((1, 1),))

    def pack(g_in, g_out, g_gain_attn, g_gain_ffn):
        pad = jnp.zeros((model_width, 2048 - attn_width - 2), jnp.float32)
        parts = [g_in, g_out, g_gain_attn[:, None], g_gain_ffn[:, None], pad]
        return jnp.concatenate([part.astype(jnp.bfloat16) for part in parts], axis=1)

    def over_shards(*partials):
        return tuple(reduce_to_owner(partial, index) for partial in partials)

    def over_replicas(gate_up, down):
        return (reduce_replicas(gate_up, replica, 1), reduce_replicas(down, replica, 0))

    grad_hidden, g_gain_ffn, g_gate_up, g_down = backward_ffn(
        kept_second, cotangent.astype(jnp.float32), weights_second
    )
    ffn_second = over_shards(g_gate_up, g_down)
    grad, g_gain_attn, g_in, g_out, _ = backward_attention(
        kept_second, grad_hidden, weights_second, tables, index
    )
    grad, ffn_second = tied(grad.astype(jnp.bfloat16), ffn_second)
    ffn_second = over_replicas(*ffn_second)
    (attn_second_sum,) = over_shards(pack(g_in, g_out, g_gain_attn, g_gain_ffn))
    grad_hidden, g_gain_ffn, g_gate_up, g_down = backward_ffn(
        kept_first, grad.astype(jnp.float32), weights_first
    )
    grad_hidden, ffn_second, attn_second_sum = tied(grad_hidden, ffn_second, attn_second_sum)
    ffn_second = tuple(reduce_sections(value, 1) for value in ffn_second)
    attn_second_sum = reduce_sections(reduce_replicas(attn_second_sum, replica, 1), 1)
    ffn_first = over_shards(g_gate_up, g_down)
    grad, g_gain_attn, g_in, g_out, (ffn_first, ffn_second, attn_second_sum) = backward_attention(
        kept_first, grad_hidden, weights_first, tables, index,
        (ffn_first, ffn_second, attn_second_sum),
    )
    ffn_first = tuple(reduce_sections(value, 0) for value in over_replicas(*ffn_first))
    (attn_first_sum,) = over_shards(pack(g_in, g_out, g_gain_attn, g_gain_ffn))
    attn_first_sum = reduce_sections(reduce_replicas(attn_first_sum, replica, 1), 0)
    quarters = ((attn_second_sum,) + ffn_second, (attn_first_sum,) + ffn_first)
    grad_low = grad.astype(jnp.bfloat16)
    grad_stayed = unfold_rows(grad_low, index, ((0, 0),))
    grad_arrived = unfold_rows(grad_low, index, ((1, 0),))
    attn_sum, gate_up_sum, down_sum = [
        gather_replicas(jnp.where(leading, first, second), replica, axis).astype(jnp.float32)
        for first, second, axis in zip(quarters[1], quarters[0], (1, 1, 0))
    ]
    ends_out = jnp.stack(
        [
            jnp.where(leading, grad_stayed, final_arrived).astype(jnp.float32),
            jnp.where(leading, grad_arrived, final_stayed).astype(jnp.float32),
        ]
    ).reshape(1, 2, 1, tok_count, model_width)
    cuts = [w_query.shape[2], w_query.shape[2] + w_key.shape[2], in_width, attn_width]
    g_query, g_key, g_value, g_out, _ = jnp.split(attn_sum, cuts, axis=1)
    units = w_gate.shape[2]
    return (
        ends_out,
        attn_sum[:, attn_width][None],
        g_query[None],
        g_key[None],
        g_value[None],
        g_out[None],
        attn_sum[:, attn_width + 1][None],
        gate_up_sum[:, :units][None],
        gate_up_sum[:, units:][None],
        down_sum[None],
    )


def solution(mesh):
    balanced = (
        mesh.shape["section"] == 2 and mesh.shape["replica"] == 4 and mesh.shape["shard"] == 4
    )
    program = both_sections if balanced else on_device
    return jax.shard_map(
        program,
        mesh=mesh,
        in_specs=(
            P("section", None, "replica", "shard", None),
            P("section", "shard"),
            P("section", "shard", None),
            P("section", "shard", None),
            P("section", "shard", None),
            P("section", "shard", None),
            P("section", "shard"),
            P("section", "shard", None),
            P("section", "shard", None),
            P("section", "shard", None),
        ),
        out_specs=(
            P("section", None, "replica", "shard", None),
            P("section", "shard"),
            P("section", "shard", None),
            P("section", "shard", None),
            P("section", "shard", None),
            P("section", "shard", None),
            P("section", "shard"),
            P("section", "shard", None),
            P("section", "shard", None),
            P("section", "shard", None),
        ),
        check_vma=False,
    )
```
